32 devices in a mesh: groups: 2 (over y), expert: 4 (over z), dp: 4 (over x, core).
Axes of the slice: x: 2, y: 2, z: 4, core: 2. Of those that a mesh axis runs over, the one named last changes fastest.
Arguments:
- tokens: bfloat16 [4096, 3584], P(('groups', 'expert', 'dp')), parts along dimension 0, may hold values from -6 to 6
- w_gate: bfloat16 [3584, 8192], P(None, 'expert'), may hold values from -0.09375 to 0.09375
- w_up: bfloat16 [3584, 8192], P(None, 'expert'), may hold values from -0.09375 to 0.09375
- w_down: bfloat16 [8192, 3584], P('expert'), may hold values from -0.125 to 0.125
- w_latent: bfloat16 [3584, 576], P('expert'), may hold values from -0.09375 to 0.09375
- latent_gain: float32 [512], replicated, may hold values from 0.1 to 1.9
- route_ids: int32 [4096, 8], P(('groups', 'expert', 'dp')), parts along dimension 0, may hold values from 0 to 255, all different within a row; in each aligned block of 128 rows (0 to 127, 128 to 255, ...) at most 8 rows name the same one
- route_weight: float32 [4096, 8], P(('groups', 'expert', 'dp')), parts along dimension 0, may hold values from 0.5 to 2
- old_latents: bfloat16 [256, 9216], P(('groups', 'expert', 'dp')), parts along dimension 0, may hold values from -6 to 6
- survive: int32 [256], P(('groups', 'expert', 'dp')), parts along dimension 0, may hold values from 0 to 1, as said below
- old_target: int32 [256], P(('groups', 'expert', 'dp')), parts along dimension 0, may hold values from -1 to 127, as said below
Outputs:
- moe_out: bfloat16 [4096, 3584], P(('groups', 'expert', 'dp')), parts along dimension 0
- latents: bfloat16 [256, 9216], P(('groups', 'expert', 'dp')), parts along dimension 0
The draws below stay inside these ranges and needn't reach their ends.
There are 2 independent parts, one for each index of `groups`. The reference program is written for one: setup_inputs(seed, part) draws one part's arguments, and reference() takes and returns one part's arrays. A program takes and returns all parts, laid end to end along the dimension named above; an argument that names none is the same for every part. Nothing has to cross between parts.
Inputs may be any that keep to these rules, and one draw needn't show every extreme that they name: `route_ids`: in each aligned block of 128 rows (the rows of one device) no expert is named more than 8 times. survive[j] = 1 exactly where some entry of old_target equals j. `old_target`: entries other than -1 are distinct; the new page of an old page lies on a device with the same dp index; of one device's pages, at most 2 go to any one device.
All inputs are finite; a program needn't handle non-finite values.
Results may differ from the reference program's by a relative error of at most 0.0085.
Values may be sent and summed in bfloat16 or wider, within the bound.
No kernel may reach another device: no remote copies, remote signals or barrier semaphores. Data moves between devices by JAX's collectives and lax.ppermute only.
A program may use at most 128 MiB of HBM per device.

```python
import math
import jax
import jax.numpy as jnp
import numpy as np
from jax import lax

D = 3584
FF = 2048
EXPERTS = 4
EXPERTS_ALL = 256
TOP = 8
KV = 512
LAT = 576
PAGE = 16
TOK_DEV = 128
CAP = 8
PAGES_DEV = 8
TOKENS = 2048
NPAGES = 128
N_EXPERT = 4
N_DP = 4


def page_plan(key):
    key_list = jax.random.split(key, 3)
    device_perm = jax.vmap(lambda sub: jax.random.permutation(sub, N_EXPERT))(jax.random.split(key_list[0], N_DP)).astype(jnp.int32)
    slot_perm = jax.vmap(lambda sub: jax.random.permutation(sub, PAGES_DEV))(jax.random.split(key_list[1], N_DP * N_EXPERT)).astype(jnp.int32)
    slot_perm = slot_perm.reshape(N_DP, N_EXPERT, PAGES_DEV)
    alive = (jax.random.randint(key_list[2], (N_DP, N_EXPERT, PAGES_DEV), 0, 4) < 3).astype(jnp.int32)
    grid_e = jnp.broadcast_to(jnp.arange(N_EXPERT, dtype=jnp.int32)[:, None, None], (N_EXPERT, N_DP, PAGES_DEV))
    grid_d = jnp.broadcast_to(jnp.arange(N_DP, dtype=jnp.int32)[None, :, None], (N_EXPERT, N_DP, PAGES_DEV))
    grid_k = jnp.broadcast_to(jnp.arange(PAGES_DEV, dtype=jnp.int32)[None, None, :], (N_EXPERT, N_DP, PAGES_DEV))
    target_dev = (device_perm[grid_d, grid_e] + grid_k) % N_EXPERT
    target_slot = slot_perm[grid_d, target_dev, grid_k]
    target_alive = alive[grid_d, target_dev, target_slot]
    target_index = (target_dev * N_DP + grid_d) * PAGES_DEV + target_slot
    old_target = jnp.where(target_alive > 0, target_index, -1).astype(jnp.int32).reshape(-1)
    survive = alive[grid_d, grid_e, grid_k].astype(jnp.int32).reshape(-1)
    return (survive, old_target)


def draw_survive(key, part):
    return page_plan(key)[0]


def draw_old_target(key, part):
    return page_plan(key)[1]


def level_of(rng, shape, shards, least, high):
    loudness, own = 1.0, jax.random.fold_in(rng, 6)
    for axis_at, parts in shards:
        steps = jnp.exp(jax.random.uniform(jax.random.fold_in(own, axis_at), (parts,), jnp.float32, least / len(shards), high / len(shards)))
        loudness = loudness * jnp.repeat(steps, shape[axis_at] // parts).reshape([-1 if axis == axis_at else 1 for axis in range(len(shape))])
    return loudness


def deal_out(key, own, number, rows, count, top, most, skew):
    ranking = jax.random.permutation(key, count)
    heavy_load, usual = portions_of(count, rows * top, most, skew, True), portions_of(count, rows * top, most, skew, False)
    places = jnp.arange(count)

    def named(lengths, offset_by):
        used = int((lengths > 0).sum())
        fixed = max(1, used // 4)
        shifted = fixed + (places - fixed + offset_by * (used - fixed)) % max(1, count - fixed)
        return jnp.zeros((count,), jnp.int32).at[ranking[jnp.where(places < fixed, places, shifted)]].set(jnp.asarray(lengths, jnp.int32))

    lengths = jnp.where(number % 4 == 0, named(heavy_load, number // 4), named(usual, number - number // 4 - 1))
    mixed = jax.random.permutation(jax.random.fold_in(own, 3), count)
    giver, sink = mixed[0:count // 2 * 2:2], mixed[1:count // 2 * 2:2]
    room = jnp.minimum(lengths[giver] - 1, most - lengths[sink]) // 2
    room = jnp.where((giver == ranking[0]) | (sink == ranking[0]) | (lengths[sink] == 0), 0, jnp.maximum(room, 0))
    shifted = jax.random.randint(jax.random.fold_in(own, 4), (count // 2,), 0, 1 << 20) % (room + 1)
    lengths = lengths.at[giver].add(-shifted).at[sink].add(shifted)
    items = jnp.searchsorted(jnp.cumsum(lengths), jnp.arange(rows * top), side="right").astype(jnp.int32)
    listing = items.reshape(top, rows).T
    listing = listing[jax.random.permutation(jax.random.fold_in(own, 1), rows)]
    offset_by = jax.random.randint(jax.random.fold_in(own, 2), (rows, 1), 0, top)
    return jnp.take_along_axis(listing, (jnp.arange(top)[None, :] + offset_by) % top, axis=1)


def portions_of(number_of, total, most, skew, full):
    portions = [(1 << 20) // math.isqrt(rank ** skew) + 1 for rank in range(1, number_of + 1)]
    largest = most if full else min(most, max(-(-total // number_of), total * portions[0] // sum(portions)))
    least = 1 if total - largest >= number_of - 1 else 0
    holding, rest = [largest] + [least] * (number_of - 1), total - largest - least * (number_of - 1)
    while rest > 0:
        free = [i for i in range(1, number_of) if holding[i] < largest] or [i for i in range(1, number_of) if holding[i] < most]
        whole, left = sum([portions[i] for i in free]), rest
        for i in free:
            addition = min(most - holding[i], max(1, left * portions[i] // whole), rest)
            holding[i] = holding[i] + addition
            rest = rest - addition
    return np.array(holding)


def centred(stream_key, dims, scale, reach, cuts=(), held_as=jnp.bfloat16):
    level = level_of(stream_key, dims, cuts, -0.22, 0.18) if cuts else 1.0
    result = jax.random.normal(stream_key, dims, jnp.float32) * scale * level
    return jnp.minimum(jnp.maximum(result, -reach), reach).astype(held_as)


def setup_inputs(seed: int = 0, part: int = 0) -> dict:
    arg_keys = jax.random.split(jax.random.key(seed), 12)
    own_keys = jax.random.split(jax.random.fold_in(arg_keys[11], part), 12)
    tokens = centred(own_keys[0], (TOKENS, D), 1.0, 6.0, ((0, 16),))
    w_gate = centred(arg_keys[1], (D, EXPERTS * FF), D ** -0.5, 0.09375, ((1, 4),))
    w_up = centred(arg_keys[2], (D, EXPERTS * FF), D ** -0.5, 0.09375, ((1, 4),))
    w_down = centred(arg_keys[3], (EXPERTS * FF, D), FF ** -0.5, 0.125, ((0, 4),))
    w_latent = centred(arg_keys[4], (D, LAT), D ** -0.5, 0.09375, ((0, 4),))
    latent_gain = jnp.clip(1.0 + 0.18 * jax.random.normal(arg_keys[5], (KV,), jnp.float32), 0.1, 1.9)
    route_ids_keys = jax.random.split(jax.random.fold_in(own_keys[6], 1), TOKENS // TOK_DEV)
    route_ids_turns = jax.random.permutation(jax.random.fold_in(own_keys[6], 3), TOKENS // TOK_DEV)
    route_ids = jax.vmap(lambda own, number: deal_out(jax.random.fold_in(own_keys[6], 2), own, number, TOK_DEV, EXPERTS_ALL, TOP, CAP, 2))(route_ids_keys, route_ids_turns).reshape((TOKENS, TOP))
    route_weight = jnp.clip(0.5 + 1.5 * jax.random.uniform(own_keys[7], (TOKENS, TOP), jnp.float32) ** level_of(own_keys[7], (TOKENS, TOP), ((0, 16),), -0.2, 0.2), 0.5, 2.0)
    old_latents = centred(own_keys[8], (NPAGES, PAGE * LAT), 1.0, 6.0, ((0, 16),))
    survive = draw_survive(jax.random.fold_in(jax.random.fold_in(arg_keys[11], part), 71), part)
    old_target = draw_old_target(jax.random.fold_in(jax.random.fold_in(arg_keys[11], part), 71), part)
    return {"tokens": tokens, "w_gate": w_gate, "w_up": w_up, "w_down": w_down, "w_latent": w_latent, "latent_gain": latent_gain, "route_ids": route_ids, "route_weight": route_weight, "old_latents": old_latents, "survive": survive, "old_target": old_target}


EPS = 1e-06

def reference(tokens, w_gate, w_up, w_down, w_latent, latent_gain, route_ids, route_weight, old_latents, survive, old_target):
    projected = jnp.dot(tokens, w_latent, preferred_element_type=jnp.float32)
    nope_part = projected[:, :KV]
    inv_rms = lax.rsqrt(lax.optimization_barrier(jnp.mean(nope_part * nope_part, axis=1, keepdims=True)) + EPS)
    rebuilt = jnp.concatenate([nope_part * inv_rms * latent_gain, projected[:, KV:]], axis=1).astype(jnp.bfloat16)
    rebuilt = rebuilt.reshape(NPAGES, PAGE * LAT)
    valid_out = old_target >= 0
    target_rows = jnp.where(valid_out, old_target, 0).astype(jnp.int32)
    sent_rows = jnp.where(valid_out[:, None], old_latents, jnp.zeros_like(old_latents))
    carried = jnp.zeros((NPAGES, PAGE * LAT), jnp.bfloat16).at[target_rows].add(sent_rows)
    latents = jnp.where((survive > 0)[:, None], carried, rebuilt)
    capacity = CAP * N_EXPERT * N_DP
    combined = jnp.zeros((TOKENS, D), jnp.float32)
    for expert in range(EXPERTS):
        chosen = route_ids == expert
        token_weight = lax.optimization_barrier(jnp.sum(jnp.where(chosen, route_weight, jnp.zeros_like(route_weight)), axis=1))
        picked = jnp.any(chosen, axis=1)
        order = jnp.argsort(jnp.where(picked, 0, 1).astype(jnp.int32), stable=True)[:capacity].astype(jnp.int32)
        row_block = jnp.take(tokens, order, axis=0)
        gate_cols = w_gate[:, expert * FF:(expert + 1) * FF]
        up_cols = w_up[:, expert * FF:(expert + 1) * FF]
        down_rows = w_down[expert * FF:(expert + 1) * FF, :]
        gate_value = jnp.dot(row_block, gate_cols, preferred_element_type=jnp.float32)
        up_value = jnp.dot(row_block, up_cols, preferred_element_type=jnp.float32)
        hidden = (jax.nn.silu(gate_value) * up_value).astype(jnp.bfloat16)
        expert_y = jnp.dot(hidden, down_rows, preferred_element_type=jnp.float32)
        combined = combined.at[order].add(expert_y * jnp.take(token_weight, order)[:, None])
    return (combined.astype(jnp.bfloat16), latents)
```

```python
import functools

import jax
import jax.numpy as jnp
from jax import lax
from jax.experimental import pallas as pl
from jax.experimental.pallas import tpu as pltpu
from jax.sharding import PartitionSpec as P

FF = 2048
EXPERTS = 4
KV = 512
CAP = 8
PER_PAIR = 2
SPLIT = 4
LANES = 128
ROWS = 16


EPS = 1e-06
VMEM = pltpu.VMEM
SMEM = pltpu.SMEM
CHUNK = 512
NT = (((1,), (1,)), ((), ()))
TN = (((0,), (0,)), ((), ()))


def xor_pairs(count, bit):
    return [(at, at ^ bit) for at in range(count)]


def plane_pairs(group_count, dp_count, core_zero_along_x):
    pairs = []
    for group in range(group_count):
        for dp in range(dp_count):
            along_x = (dp % 2 == 0) == core_zero_along_x
            to_group, to_dp = (group, dp ^ 2) if along_x else (group ^ 1, dp)
            pairs.append((group * dp_count + dp, to_group * dp_count + to_dp))
    return pairs


def piece_rows(width):
    chip = width // 4
    core = -(-(chip // 2) // ROWS) * ROWS
    return chip, core


def open_kernel(page_span, *refs):
    sources, latent_ref, outs = refs[:5], refs[5], refs[6:]
    sends, mixing_ref, pages = outs[:EXPERTS], outs[EXPERTS], outs[EXPERTS + 1 : 2 * EXPERTS + 1]
    piece_ref, across_ref = outs[2 * EXPERTS + 1 : 2 * EXPERTS + 3]
    *held, sem, sems = outs[2 * EXPERTS + 3 :]
    ids_ref, weight_ref, tokens_ref, old_ref, target_ref = held
    copies = [
        pltpu.make_async_copy(source, target, sems.at[at])
        for at, (source, target) in enumerate(zip(sources, held))
    ]
    for copy in copies:
        copy.start()
    group, me, dp = (lax.axis_index(axis) for axis in ("groups", "expert", "dp"))
    chip_rows, core_rows = piece_rows(latent_ref.shape[0])
    start = (group * 2 + dp // 2) * chip_rows + (dp % 2) * (chip_rows - core_rows)
    piece = pltpu.make_async_copy(
        latent_ref.at[pl.ds(pl.multiple_of(start, ROWS), core_rows)], piece_ref, sem
    )
    piece.start()
    for copy in copies:
        copy.wait()
    shard = latent_ref.shape[1]
    for half, bit in enumerate((1, 3)):
        columns = pl.ds(pl.multiple_of((me ^ bit) * shard, LANES), shard)
        across_ref[:, half * shard : (half + 1) * shard] = tokens_ref[:, columns]
    top_count, token_count = ids_ref.shape
    slot_count = EXPERTS * CAP
    row = lax.broadcasted_iota(jnp.int32, (slot_count, token_count), 0)
    expert_of = (row >> 3) ^ me
    chosen = jnp.zeros((slot_count, token_count), jnp.float32)
    weight = jnp.zeros((slot_count, token_count), jnp.float32)
    for at in range(top_count):
        named = ids_ref[at : at + 1, :] == expert_of
        chosen = jnp.where(named, 1.0, chosen)
        weight = jnp.where(named, weight_ref[at : at + 1, :], weight)
    before = lax.broadcasted_iota(jnp.int32, (token_count, token_count), 0)
    token = lax.broadcasted_iota(jnp.int32, (token_count, token_count), 1)
    earlier = jnp.where(before < token, 1.0, 0.0).astype(jnp.bfloat16)
    rank = jnp.dot(chosen.astype(jnp.bfloat16), earlier, preferred_element_type=jnp.float32)
    placed = jnp.where(rank == (row & 7).astype(jnp.float32), chosen, 0.0)
    mixing_ref[...] = placed * weight
    outgoing = jnp.dot(
        placed.astype(jnp.bfloat16), tokens_ref[...], preferred_element_type=jnp.float32
    )
    for at in range(EXPERTS):
        sends[at][...] = outgoing[at * CAP : (at + 1) * CAP].astype(jnp.bfloat16)
    page_count, width = old_ref.shape
    row_count = EXPERTS * PER_PAIR * SPLIT
    out_row = lax.broadcasted_iota(jnp.int32, (row_count, page_count), 0)
    old_page = lax.broadcasted_iota(jnp.int32, (row_count, page_count), 1)
    tag_row = lax.broadcasted_iota(jnp.int32, (row_count, LANES), 0)
    select = [jnp.zeros((row_count, page_count), jnp.float32) for _ in range(SPLIT)]
    tags = jnp.zeros((row_count, LANES), jnp.float32)
    targets = [target_ref[at] for at in range(page_count)]
    peers = [jnp.where(target >= 0, target // page_span, -1) for target in targets]
    for at in range(page_count):
        rank_at = jnp.int32(0)
        for first in range(at):
            rank_at = rank_at + jnp.where(peers[first] == peers[at], 1, 0)
        row_at = ((peers[at] ^ me) * PER_PAIR + rank_at) * SPLIT
        row_at = jnp.where(peers[at] >= 0, row_at, -SPLIT)
        for part in range(SPLIT):
            here = (out_row == row_at + part) & (old_page == at)
            select[part] = jnp.where(here, 1.0, select[part])
        slot_tag = (targets[at] % page_count + 1).astype(jnp.float32)
        tags = jnp.where((tag_row >= row_at) & (tag_row < row_at + SPLIT), slot_tag, tags)
    width = width // SPLIT
    moved = jnp.zeros((row_count, width), jnp.float32)
    for part in range(SPLIT):
        columns = slice(part * width, (part + 1) * width)
        moved = moved + jnp.dot(
            select[part].astype(jnp.bfloat16),
            old_ref[:, columns],
            preferred_element_type=jnp.float32,
        )
    for at in range(EXPERTS):
        rows = slice(at * PER_PAIR * SPLIT, (at + 1) * PER_PAIR * SPLIT)
        pages[at][:, :width] = moved[rows].astype(jnp.bfloat16)
        pages[at][:, width:] = tags[rows].astype(jnp.bfloat16)
    piece.wait()


def open_work(ids, weights, tokens, old_latents, latent, old_target):
    token_count, model_width = tokens.shape
    page_count, page_width = old_latents.shape
    send = jax.ShapeDtypeStruct((CAP, model_width), jnp.bfloat16)
    mixing = jax.ShapeDtypeStruct((EXPERTS * CAP, token_count), jnp.float32)
    page = jax.ShapeDtypeStruct((PER_PAIR * SPLIT, page_width // SPLIT + LANES), jnp.bfloat16)
    piece = jax.ShapeDtypeStruct((piece_rows(latent.shape[0])[1], latent.shape[1]), jnp.bfloat16)
    across = jax.ShapeDtypeStruct((token_count, 2 * latent.shape[1]), jnp.bfloat16)
    spec = pl.BlockSpec(memory_space=VMEM)
    inputs = [
        pltpu.with_memory_space_constraint(value, pltpu.HBM)
        for value in (ids, weights, tokens, old_latents, old_target, latent)
    ]
    results = pl.pallas_call(
        functools.partial(open_kernel, page_count * lax.axis_size("dp")),
        out_shape=(send,) * EXPERTS + (mixing,) + (page,) * EXPERTS + (piece, across),
        in_specs=[pl.BlockSpec(memory_space=pltpu.HBM)] * 6,
        out_specs=(spec,) * (2 * EXPERTS + 3),
        scratch_shapes=[VMEM(value.shape, value.dtype) for value in inputs[:4]]
        + [
            SMEM(old_target.shape, old_target.dtype),
            pltpu.SemaphoreType.DMA,
            pltpu.SemaphoreType.DMA((5,)),
        ],
        compiler_params=pltpu.CompilerParams(vmem_limit_bytes=8 << 20),
        cost_estimate=pl.CostEstimate(
            flops=20_000_000_000, bytes_accessed=2 << 20, transcendentals=0
        ),
        name="open",
    )(*inputs)
    sends, mixing, rest = results[:EXPERTS], results[EXPERTS], results[EXPERTS + 1 :]
    return sends, mixing, rest[:EXPERTS], rest[EXPERTS], rest[EXPERTS + 1]


def stacked_rows(refs):
    return jnp.concatenate([ref[...].astype(jnp.float32) for ref in refs], axis=0).astype(
        jnp.bfloat16
    )


def gate_up_kernel(*refs):
    rows, (gate_ref, up_ref) = refs[:EXPERTS], refs[EXPERTS : EXPERTS + 2]
    hidden_ref = refs[-1]
    block = stacked_rows(rows)
    step = CHUNK // 2
    for at in range(0, gate_ref.shape[1], step):
        columns = slice(at, at + step)
        gate = jnp.dot(block, gate_ref[:, columns], preferred_element_type=jnp.float32)
        up = jnp.dot(block, up_ref[:, columns], preferred_element_type=jnp.float32)
        hidden_ref[:, columns] = (gate / (1.0 + jnp.exp(-gate)) * up).astype(jnp.bfloat16)


def gate_up(rows, w_gate, w_up, after):
    spec, unread = pl.BlockSpec(memory_space=VMEM), pl.BlockSpec(memory_space=pl.ANY)
    held = [pltpu.with_memory_space_constraint(w, VMEM) for w in (w_gate, w_up)]
    model_width, unit_count = w_gate.shape
    row_count = EXPERTS * CAP
    return pl.pallas_call(
        gate_up_kernel,
        out_shape=jax.ShapeDtypeStruct((row_count, unit_count), jnp.bfloat16),
        in_specs=[spec] * (EXPERTS + 2) + [unread] * len(after),
        out_specs=spec,
        compiler_params=pltpu.CompilerParams(vmem_limit_bytes=4 << 20),
        cost_estimate=pl.CostEstimate(
            flops=4 * row_count * model_width * unit_count,
            bytes_accessed=4 * model_width * unit_count,
            transcendentals=row_count * unit_count,
        ),
        name="gate_up",
    )(*rows, *held, *after)


def down_kernel(hidden_ref, down_ref, *refs):
    pages, outs = refs[:EXPERTS], refs[-EXPERTS:]
    model_width = down_ref.shape[1]
    for peer in range(EXPERTS):
        outs[peer][:, model_width:] = pages[peer][...]
    for at in range(0, down_ref.shape[1], CHUNK):
        columns = slice(at, at + CHUNK)
        result = jnp.dot(
            hidden_ref[...], down_ref[:, columns], preferred_element_type=jnp.float32
        )
        for peer in range(EXPERTS):
            part = result[peer * CAP : (peer + 1) * CAP]
            outs[peer][:, columns] = part.astype(jnp.bfloat16)


def down(hidden, w_down, pages, after):
    spec, unread = pl.BlockSpec(memory_space=VMEM), pl.BlockSpec(memory_space=pl.ANY)
    unit_count, model_width = w_down.shape
    return pl.pallas_call(
        down_kernel,
        out_shape=(jax.ShapeDtypeStruct((CAP, model_width + pages[0].shape[1]), jnp.bfloat16),)
        * EXPERTS,
        in_specs=[spec] * (2 + EXPERTS) + [unread] * len(after),
        out_specs=(spec,) * EXPERTS,
        compiler_params=pltpu.CompilerParams(vmem_limit_bytes=4 << 20),
        cost_estimate=pl.CostEstimate(
            flops=2 * EXPERTS * CAP * model_width * unit_count,
            bytes_accessed=2 * model_width * unit_count,
            transcendentals=0,
        ),
        name="down",
    )(hidden, pltpu.with_memory_space_constraint(w_down, VMEM), *pages, *after)


def combine_kernel(mixing_ref, *refs):
    rows, out_ref = refs[:EXPERTS], refs[EXPERTS]
    block = stacked_rows(rows)
    mixing = mixing_ref[...]
    high = mixing.astype(jnp.bfloat16).astype(jnp.float32)
    mixing = jnp.concatenate([high, mixing - high], axis=0).astype(jnp.bfloat16)
    block = jnp.concatenate([block, block], axis=0)
    total = lax.dot_general(mixing, block, TN, preferred_element_type=jnp.float32)
    out_ref[...] = total.astype(jnp.bfloat16)


def combine(mixing, rows, model_width):
    slot_count, token_count = mixing.shape
    width = model_width // 2
    columns = pl.BlockSpec((CAP, width), lambda at: (0, at))
    return pl.pallas_call(
        combine_kernel,
        grid=(model_width // width,),
        out_shape=jax.ShapeDtypeStruct((token_count, model_width), jnp.bfloat16),
        in_specs=[pl.BlockSpec((slot_count, token_count), lambda at: (0, 0))] + [columns] * EXPERTS,
        out_specs=pl.BlockSpec((token_count, width), lambda at: (0, at)),
        compiler_params=pltpu.CompilerParams(vmem_limit_bytes=8 << 20),
        cost_estimate=pl.CostEstimate(
            flops=4 * token_count * slot_count * model_width,
            bytes_accessed=3 * token_count * model_width,
            transcendentals=0,
        ),
        name="combine",
    )(mixing, *rows)


def project_kernel(tokens_ref, theirs_ref, own_ref, *refs):
    held, (mine_out, theirs_out), (far_ref, sems) = refs[:4], refs[-4:-2], refs[-2:]
    group, me, dp = (lax.axis_index(axis) for axis in ("groups", "expert", "dp"))
    shard = own_ref.shape[1]
    chip_rows, core_rows = piece_rows(own_ref.shape[0])
    chip, core = group * 2 + dp // 2, dp % 2

    def copies_of(my_core):
        copies = []
        for which in range(2):
            core_at = my_core if which == 0 else 1 - my_core
            near_xor = 1 if core_at == 0 else 2
            for at, chip_xor in enumerate((0, near_xor, 3 - near_xor, 3)):
                buffer = held[2 * which + at // 2].at[at % 2]
                skip = 0 if core_at == 0 else 2 * core_rows - chip_rows
                start = (chip ^ chip_xor) * chip_rows + (0 if core_at == 0 else core_rows)
                count = core_rows - skip
                copies.append(
                    pltpu.make_async_copy(
                        buffer.at[pl.ds(skip, count)],
                        far_ref.at[pl.ds(pl.multiple_of(start, ROWS), count)],
                        sems.at[len(copies)],
                    )
                )
        return copies

    def on_each_core(act):
        for my_core in range(2):

            @pl.when(core == my_core)
            def _(my_core=my_core):
                for copy in copies_of(my_core):
                    act(copy)

    def part(left, weights_ref):
        return lax.dot_general(left, weights_ref[...], NT, preferred_element_type=jnp.float32)

    on_each_core(lambda copy: copy.start())
    theirs_near = part(theirs_ref[:, :shard], own_ref)
    mine_near = part(tokens_ref[:, pl.ds(pl.multiple_of(me * shard, LANES), shard)], own_ref)
    on_each_core(lambda copy: copy.wait())
    theirs_far = part(theirs_ref[:, shard:], far_ref)
    theirs_out[...] = (theirs_near + theirs_far).astype(jnp.bfloat16)
    far_columns = pl.ds(pl.multiple_of((me ^ 2) * shard, LANES), shard)
    mine_out[...] = mine_near + part(tokens_ref[:, far_columns], far_ref)


def project(tokens, theirs, own, held, after):
    vmem, hbm = pl.BlockSpec(memory_space=VMEM), pl.BlockSpec(memory_space=pl.ANY)
    token_count = tokens.shape[0]
    width, shard = own.shape
    return pl.pallas_call(
        project_kernel,
        out_shape=(
            jax.ShapeDtypeStruct((token_count, width), jnp.float32),
            jax.ShapeDtypeStruct((token_count, width), jnp.bfloat16),
        ),
        in_specs=[vmem] * 3 + [hbm] * (4 + len(after)),
        out_specs=(vmem, vmem),
        scratch_shapes=[VMEM((width, shard), jnp.bfloat16), pltpu.SemaphoreType.DMA((8,))],
        compiler_params=pltpu.CompilerParams(vmem_limit_bytes=8 << 20),
        cost_estimate=pl.CostEstimate(
            flops=8 * token_count * shard * width, bytes_accessed=4 << 20, transcendentals=0
        ),
        name="project",
    )(tokens, theirs, own, *held, *after)


def finish_kernel(mine_ref, theirs_ref, gain_ref, survive_ref, *refs):
    arrived, out_ref = refs[:EXPERTS], refs[EXPERTS]
    page_count, page_width = out_ref.shape
    projected = mine_ref[...] + theirs_ref[...].astype(jnp.float32)
    nope_part = projected[:, :KV]
    inv_rms = lax.rsqrt(jnp.mean(nope_part * nope_part, axis=1, keepdims=True) + EPS)
    rebuilt = jnp.concatenate([nope_part * inv_rms * gain_ref[...], projected[:, KV:]], axis=1)
    rebuilt = rebuilt.astype(jnp.bfloat16)
    token_count, width = rebuilt.shape
    page_tokens = token_count // page_count
    row = lax.broadcasted_iota(jnp.int32, (token_count, token_count), 0)
    source = lax.broadcasted_iota(jnp.int32, (token_count, token_count), 1)
    moves = source == (row % page_count) * page_tokens + row // page_count
    ordered = jnp.dot(
        jnp.where(moves, 1.0, 0.0).astype(jnp.bfloat16),
        rebuilt,
        preferred_element_type=jnp.float32,
    )
    columns = slice(arrived[0].shape[1] - LANES - page_width // SPLIT, None)
    arrivals = jnp.concatenate([ref[:, columns].astype(jnp.float32) for ref in arrived], axis=0)
    part_width = page_width // SPLIT
    row_count = arrivals.shape[0]
    slot = lax.broadcasted_iota(jnp.int32, (row_count, page_count), 1).astype(jnp.float32)
    part_of = lax.broadcasted_iota(jnp.int32, (row_count, page_count), 0) % SPLIT
    meant = arrivals[:, part_width : part_width + 1] == slot + 1.0
    arrivals = arrivals[:, :part_width].astype(jnp.bfloat16)
    carried = [
        lax.dot_general(
            jnp.where(meant & (part_of == part), 1.0, 0.0).astype(jnp.bfloat16),
            arrivals,
            TN,
            preferred_element_type=jnp.float32,
        )
        for part in range(SPLIT)
    ]
    page_row = lax.broadcasted_iota(jnp.int32, (page_count, 2 * width), 0)
    survives = jnp.zeros((page_count, 2 * width), jnp.int32)
    for at in range(page_count):
        survives = jnp.where(page_row == at, survive_ref[at], survives)
    for at in range(0, page_tokens, 2):
        fresh = jnp.concatenate(
            [ordered[(at + half) * page_count : (at + half + 1) * page_count] for half in range(2)],
            axis=1,
        )
        columns = slice(at * width, (at + 2) * width)
        start = at * width % part_width
        kept = carried[at * width // part_width][:, start : start + 2 * width]
        chosen = jnp.where(survives > 0, kept, fresh)
        out_ref[:, columns] = chosen.astype(jnp.bfloat16)


def finish(mine, theirs, latent_gain, survive, arrived, page_count, page_width):
    vmem = pl.BlockSpec(memory_space=VMEM)
    return pl.pallas_call(
        finish_kernel,
        out_shape=jax.ShapeDtypeStruct((page_count, page_width), jnp.bfloat16),
        in_specs=[vmem] * 3 + [pl.BlockSpec(memory_space=SMEM)] + [vmem] * EXPERTS,
        out_specs=vmem,
        compiler_params=pltpu.CompilerParams(vmem_limit_bytes=6 << 20),
        cost_estimate=pl.CostEstimate(
            flops=4 * mine.shape[0] ** 2 * mine.shape[1],
            bytes_accessed=1 << 20,
            transcendentals=mine.shape[0],
        ),
        name="finish",
    )(mine, theirs, latent_gain.reshape(1, -1), survive, *arrived)


def swap(value, axis, bit):
    return lax.ppermute(value, axis, xor_pairs(lax.axis_size(axis), bit))


def tied(value, *after):
    return lax.optimization_barrier((value, *after))[0]


def exchanged(values, axis="expert"):
    return [values[0]] + [swap(values[bit], axis, bit) for bit in range(1, len(values))]


def block_shards(
    tokens,
    w_gate,
    w_up,
    w_down,
    w_latent,
    latent_gain,
    route_ids,
    route_weight,
    old_latents,
    survive,
    old_target,
):
    group_count, dp_count = lax.axis_size("groups"), lax.axis_size("dp")
    plane = ("groups", "dp")
    latent = w_latent.T
    sends, mixing, pages, piece, across = open_work(
        route_ids.T, route_weight.T, tokens, old_latents, latent, old_target
    )
    far_piece = swap(piece, "expert", 2)
    received = exchanged(sends)
    far_piece = tied(far_piece, received[1])
    first = lax.ppermute(far_piece, plane, plane_pairs(group_count, dp_count, True))
    theirs = swap(tied(across, *received[1:]), "expert", 1)
    hidden = gate_up(received, w_gate, w_up, (far_piece,))
    near = tied(jnp.stack([far_piece, first]), hidden)
    far = lax.ppermute(near, plane, plane_pairs(group_count, dp_count, False))
    near_other = swap(near, "dp", 1)
    results = down(hidden, w_down, pages, (near,))
    returned = exchanged(results)
    far_other = swap(far, "dp", 1)
    mine, across_sums = project(
        tokens, theirs, latent, (near, far, near_other, far_other), (results[0],)
    )
    their_sums = swap(across_sums, "expert", 1)
    moe_out = combine(mixing, returned, tokens.shape[1])
    latents = finish(mine, their_sums, latent_gain, survive, returned, *old_latents.shape)
    return (moe_out, latents)


def rebuild_latents(tokens, w_latent, latent_gain):
    projected = jnp.dot(
        tokens,
        lax.all_gather(w_latent, "expert", axis=0, tiled=True),
        preferred_element_type=jnp.float32,
    )
    nope_part = projected[:, :KV]
    inv_rms = lax.rsqrt(jnp.mean(nope_part * nope_part, axis=1, keepdims=True) + EPS)
    return jnp.concatenate([nope_part * inv_rms * latent_gain, projected[:, KV:]], axis=1).astype(
        jnp.bfloat16
    )


def moved_pages(old_latents, survive, old_target, rebuilt):
    peer_count = lax.axis_size("expert")
    dp_count = lax.axis_size("dp")
    page_count = old_latents.shape[0]
    per_pair = max(1, page_count // peer_count)
    slot_ids = jnp.arange(page_count, dtype=jnp.int32)
    peer_ids = jnp.arange(peer_count, dtype=jnp.int32)
    rank_ids = jnp.arange(per_pair, dtype=jnp.int32)
    valid_out = old_target >= 0
    target_peer = old_target // page_count // dp_count
    target_slot = jnp.where(valid_out, old_target % page_count + 1, 0).astype(jnp.float32)
    same_peer = (target_peer[:, None] == target_peer[None, :]) & valid_out[None, :]
    earlier = slot_ids[None, :] < slot_ids[:, None]
    out_rank = jnp.sum((same_peer & earlier).astype(jnp.int32), axis=1)
    select = (
        valid_out[None, None, :]
        & (target_peer[None, None, :] == peer_ids[:, None, None])
        & (out_rank[None, None, :] == rank_ids[None, :, None])
    )
    select = select.reshape(peer_count * per_pair, page_count)
    outgoing = jnp.dot(
        select.astype(jnp.bfloat16), old_latents, preferred_element_type=jnp.float32
    ).astype(jnp.bfloat16)
    slot_tags = jnp.dot(
        select.astype(jnp.float32), target_slot, precision=lax.Precision.HIGHEST
    ).astype(jnp.bfloat16)
    arrived, arrived_tags = (
        lax.all_to_all(
            outgoing.reshape(peer_count, per_pair, -1),
            "expert",
            split_axis=0,
            concat_axis=0,
            tiled=True,
        ),
        lax.all_to_all(
            slot_tags.reshape(peer_count, per_pair),
            "expert",
            split_axis=0,
            concat_axis=0,
            tiled=True,
        ),
    )
    tag_values = arrived_tags.reshape(peer_count * per_pair).astype(jnp.float32)
    chooser = (tag_values[None, :] == (slot_ids + 1).astype(jnp.float32)[:, None]).astype(
        jnp.bfloat16
    )
    carried = jnp.dot(
        chooser, arrived.reshape(peer_count * per_pair, -1), preferred_element_type=jnp.float32
    ).astype(jnp.bfloat16)
    return jnp.where((survive > 0)[:, None], carried, rebuilt)


def route_tables(route_ids, route_weight):
    token_count, top_count = route_ids.shape
    flat_ids = route_ids.reshape(-1)
    onehot = (flat_ids[:, None] == jnp.arange(EXPERTS, dtype=jnp.int32)[None, :]).astype(jnp.int32)
    slot_rank = jnp.sum((jnp.cumsum(onehot, axis=0) - onehot) * onehot, axis=1)
    slot_index = jnp.where(flat_ids < EXPERTS, flat_ids * CAP + slot_rank, -1)
    matches = slot_index[:, None] == jnp.arange(EXPERTS * CAP, dtype=jnp.int32)[None, :]
    matches = matches.reshape(token_count, top_count, EXPERTS * CAP)
    placing = jnp.sum(matches.astype(jnp.float32), axis=1).astype(jnp.bfloat16)
    mixing = jnp.sum(matches.astype(jnp.float32) * route_weight[:, :, None], axis=1)
    return (placing, mixing)


def expert_rows(received, w_gate, w_up, w_down, per_dev):
    unit_count = w_gate.shape[1] // per_dev
    gate_w = w_gate.reshape(w_gate.shape[0], per_dev, unit_count)
    up_w = w_up.reshape(w_up.shape[0], per_dev, unit_count)
    down_w = w_down.reshape(per_dev, unit_count, w_down.shape[1])
    gate_value = jnp.einsum("spkd,dpf->spkf", received, gate_w, preferred_element_type=jnp.float32)
    up_value = jnp.einsum("spkd,dpf->spkf", received, up_w, preferred_element_type=jnp.float32)
    hidden = (jax.nn.silu(gate_value) * up_value).astype(jnp.bfloat16)
    return jnp.einsum("spkf,pfd->spkd", hidden, down_w, preferred_element_type=jnp.float32)


def shards(
    tokens,
    w_gate,
    w_up,
    w_down,
    w_latent,
    latent_gain,
    route_ids,
    route_weight,
    old_latents,
    survive,
    old_target,
):
    rebuilt = rebuild_latents(tokens, w_latent, latent_gain).reshape(old_latents.shape[0], -1)
    latents = moved_pages(old_latents, survive, old_target, rebuilt)
    column_count = w_gate.shape[1]
    per_dev = max(1, column_count // FF)
    span_size = max(1, FF // column_count)
    group_count = EXPERTS // per_dev
    model_width = tokens.shape[1]
    placing, mixing = route_tables(route_ids, route_weight)
    outgoing = jnp.einsum("te,td->ed", placing, tokens, preferred_element_type=jnp.float32).astype(
        jnp.bfloat16
    )
    grouped = outgoing.reshape(group_count, per_dev, CAP, model_width)
    sent_rows = jnp.repeat(grouped, span_size, axis=0)
    partial_value = expert_rows(
        lax.all_to_all(sent_rows, "expert", split_axis=0, concat_axis=0, tiled=True),
        w_gate,
        w_up,
        w_down,
        per_dev,
    )
    returned = lax.all_to_all(
        partial_value.astype(jnp.bfloat16), "expert", split_axis=0, concat_axis=0, tiled=True
    ).astype(partial_value.dtype)
    summed = jnp.sum(returned.reshape(group_count, span_size, per_dev, CAP, model_width), axis=1)
    expert_out = summed.reshape(EXPERTS * CAP, model_width)
    moe_out = jnp.dot(mixing, expert_out, precision=lax.Precision.HIGHEST).astype(jnp.bfloat16)
    return (moe_out, latents)


def small_block(mesh):
    sizes = (mesh.shape["groups"], mesh.shape["expert"], mesh.shape["dp"])
    return sizes == (2, EXPERTS, 4)


def solution(mesh):
    in_specs = (
        P(("groups", "expert", "dp"), None),
        P(None, "expert"),
        P(None, "expert"),
        P("expert", None),
        P("expert", None),
        P(),
        P(("groups", "expert", "dp"), None),
        P(("groups", "expert", "dp"), None),
        P(("groups", "expert", "dp"), None),
        P(("groups", "expert", "dp")),
        P(("groups", "expert", "dp")),
    )
    out_specs = (P(("groups", "expert", "dp"), None), P(("groups", "expert", "dp"), None))
    body = block_shards if small_block(mesh) else shards
    return jax.shard_map(body, mesh=mesh, in_specs=in_specs, out_specs=out_specs, check_vma=False)
```

```python
import functools

import jax
import jax.numpy as jnp
from jax import lax
from jax.experimental import pallas as pl
from jax.experimental.pallas import tpu as pltpu
from jax.sharding import PartitionSpec as P

FF = 2048
EXPERTS = 4
KV = 512
CAP = 8
PER_PAIR = 2
SPLIT = 4
LANES = 128
ROWS = 16


EPS = 1e-06
VMEM = pltpu.VMEM
SMEM = pltpu.SMEM
CHUNK = 512
NT = (((1,), (1,)), ((), ()))
TN = (((0,), (0,)), ((), ()))


def xor_pairs(count, bit):
    return [(at, at ^ bit) for at in range(count)]


def plane_pairs(group_count, dp_count, core_zero_along_x):
    pairs = []
    for group in range(group_count):
        for dp in range(dp_count):
            along_x = (dp % 2 == 0) == core_zero_along_x
            to_group, to_dp = (group, dp ^ 2) if along_x else (group ^ 1, dp)
            pairs.append((group * dp_count + dp, to_group * dp_count + to_dp))
    return pairs


def piece_rows(width):
    chip = width // 4
    core = -(-(chip // 2) // ROWS) * ROWS
    return chip, core


def cut_kernel(latent_ref, piece_ref, sem):
    group, dp = lax.axis_index("groups"), lax.axis_index("dp")
    chip_rows, core_rows = piece_rows(latent_ref.shape[0])
    start = (group * 2 + dp // 2) * chip_rows + (dp % 2) * (chip_rows - core_rows)
    piece = pltpu.make_async_copy(
        latent_ref.at[pl.ds(pl.multiple_of(start, ROWS), core_rows)], piece_ref, sem
    )
    piece.start()
    piece.wait()


def cut(latent):
    width, shard = latent.shape
    return pl.pallas_call(
        cut_kernel,
        out_shape=jax.ShapeDtypeStruct((piece_rows(width)[1], shard), jnp.bfloat16),
        in_specs=[pl.BlockSpec(memory_space=pltpu.HBM)],
        out_specs=pl.BlockSpec(memory_space=VMEM),
        scratch_shapes=[pltpu.SemaphoreType.DMA],
        compiler_params=pltpu.CompilerParams(vmem_limit_bytes=1 << 20),
        name="cut",
    )(pltpu.with_memory_space_constraint(latent, pltpu.HBM))


def open_kernel(page_span, *refs):
    sources, outs = refs[:5], refs[5:]
    sends, mixing_ref, pages = outs[:EXPERTS], outs[EXPERTS], outs[EXPERTS + 1 : 2 * EXPERTS + 1]
    across_ref = outs[2 * EXPERTS + 1]
    *held, sems = outs[2 * EXPERTS + 2 :]
    ids_ref, weight_ref, tokens_ref, old_ref, target_ref = held
    copies = [
        pltpu.make_async_copy(source, target, sems.at[at])
        for at, (source, target) in enumerate(zip(sources, held))
    ]
    for copy in copies:
        copy.start()
    me = lax.axis_index("expert")
    for copy in copies:
        copy.wait()
    shard = across_ref.shape[1] // 2
    for half, bit in enumerate((1, 3)):
        columns = pl.ds(pl.multiple_of((me ^ bit) * shard, LANES), shard)
        across_ref[:, half * shard : (half + 1) * shard] = tokens_ref[:, columns]
    top_count, token_count = ids_ref.shape
    slot_count = EXPERTS * CAP
    row = lax.broadcasted_iota(jnp.int32, (slot_count, token_count), 0)
    expert_of = (row >> 3) ^ me
    chosen = jnp.zeros((slot_count, token_count), jnp.float32)
    weight = jnp.zeros((slot_count, token_count), jnp.float32)
    for at in range(top_count):
        named = ids_ref[at : at + 1, :] == expert_of
        chosen = jnp.where(named, 1.0, chosen)
        weight = jnp.where(named, weight_ref[at : at + 1, :], weight)
    before = lax.broadcasted_iota(jnp.int32, (token_count, token_count), 0)
    token = lax.broadcasted_iota(jnp.int32, (token_count, token_count), 1)
    earlier = jnp.where(before < token, 1.0, 0.0).astype(jnp.bfloat16)
    rank = jnp.dot(chosen.astype(jnp.bfloat16), earlier, preferred_element_type=jnp.float32)
    placed = jnp.where(rank == (row & 7).astype(jnp.float32), chosen, 0.0)
    mixing_ref[...] = placed * weight
    outgoing = jnp.dot(
        placed.astype(jnp.bfloat16), tokens_ref[...], preferred_element_type=jnp.float32
    )
    for at in range(EXPERTS):
        sends[at][...] = outgoing[at * CAP : (at + 1) * CAP].astype(jnp.bfloat16)
    page_count, width = old_ref.shape
    row_count = EXPERTS * PER_PAIR * SPLIT
    out_row = lax.broadcasted_iota(jnp.int32, (row_count, page_count), 0)
    old_page = lax.broadcasted_iota(jnp.int32, (row_count, page_count), 1)
    tag_row = lax.broadcasted_iota(jnp.int32, (row_count, LANES), 0)
    select = [jnp.zeros((row_count, page_count), jnp.float32) for _ in range(SPLIT)]
    tags = jnp.zeros((row_count, LANES), jnp.float32)
    targets = [target_ref[at] for at in range(page_count)]
    peers = [jnp.where(target >= 0, target // page_span, -1) for target in targets]
    for at in range(page_count):
        rank_at = jnp.int32(0)
        for first in range(at):
            rank_at = rank_at + jnp.where(peers[first] == peers[at], 1, 0)
        row_at = ((peers[at] ^ me) * PER_PAIR + rank_at) * SPLIT
        row_at = jnp.where(peers[at] >= 0, row_at, -SPLIT)
        for part in range(SPLIT):
            here = (out_row == row_at + part) & (old_page == at)
            select[part] = jnp.where(here, 1.0, select[part])
        slot_tag = (targets[at] % page_count + 1).astype(jnp.float32)
        tags = jnp.where((tag_row >= row_at) & (tag_row < row_at + SPLIT), slot_tag, tags)
    width = width // SPLIT
    moved = jnp.zeros((row_count, width), jnp.float32)
    for part in range(SPLIT):
        columns = slice(part * width, (part + 1) * width)
        moved = moved + jnp.dot(
            select[part].astype(jnp.bfloat16),
            old_ref[:, columns],
            preferred_element_type=jnp.float32,
        )
    for at in range(EXPERTS):
        rows = slice(at * PER_PAIR * SPLIT, (at + 1) * PER_PAIR * SPLIT)
        pages[at][:, :width] = moved[rows].astype(jnp.bfloat16)
        pages[at][:, width:] = tags[rows].astype(jnp.bfloat16)


def open_work(ids, weights, tokens, old_latents, old_target, shard):
    token_count, model_width = tokens.shape
    page_count, page_width = old_latents.shape
    send = jax.ShapeDtypeStruct((CAP, model_width), jnp.bfloat16)
    mixing = jax.ShapeDtypeStruct((EXPERTS * CAP, token_count), jnp.float32)
    page = jax.ShapeDtypeStruct((PER_PAIR * SPLIT, page_width // SPLIT + LANES), jnp.bfloat16)
    across = jax.ShapeDtypeStruct((token_count, 2 * shard), jnp.bfloat16)
    spec = pl.BlockSpec(memory_space=VMEM)
    inputs = [
        pltpu.with_memory_space_constraint(value, pltpu.HBM)
        for value in (ids, weights, tokens, old_latents, old_target)
    ]
    results = pl.pallas_call(
        functools.partial(open_kernel, page_count * lax.axis_size("dp")),
        out_shape=(send,) * EXPERTS + (mixing,) + (page,) * EXPERTS + (across,),
        in_specs=[pl.BlockSpec(memory_space=pltpu.HBM)] * 5,
        out_specs=(spec,) * (2 * EXPERTS + 2),
        scratch_shapes=[VMEM(value.shape, value.dtype) for value in inputs[:4]]
        + [
            SMEM(old_target.shape, old_target.dtype),
            pltpu.SemaphoreType.DMA((5,)),
        ],
        compiler_params=pltpu.CompilerParams(vmem_limit_bytes=8 << 20),
        cost_estimate=pl.CostEstimate(
            flops=20_000_000_000, bytes_accessed=2 << 20, transcendentals=0
        ),
        name="open",
    )(*inputs)
    sends, mixing, rest = results[:EXPERTS], results[EXPERTS], results[EXPERTS + 1 :]
    return sends, mixing, rest[:EXPERTS], rest[EXPERTS]


def stacked_rows(refs):
    return jnp.concatenate([ref[...].astype(jnp.float32) for ref in refs], axis=0).astype(
        jnp.bfloat16
    )


def gate_kernel(*refs):
    rows, gate_ref, out_ref = refs[:EXPERTS], refs[EXPERTS], refs[-1]
    block = stacked_rows(rows)
    for at in range(0, gate_ref.shape[1], CHUNK):
        columns = slice(at, at + CHUNK)
        out_ref[:, columns] = jnp.dot(
            block, gate_ref[:, columns], preferred_element_type=jnp.float32
        )


def gates(rows, w_gate, after):
    spec, unread = pl.BlockSpec(memory_space=VMEM), pl.BlockSpec(memory_space=pl.ANY)
    model_width, unit_count = w_gate.shape
    row_count = EXPERTS * CAP
    return pl.pallas_call(
        gate_kernel,
        out_shape=jax.ShapeDtypeStruct((row_count, unit_count), jnp.float32),
        in_specs=[spec] * (EXPERTS + 1) + [unread] * len(after),
        out_specs=spec,
        compiler_params=pltpu.CompilerParams(vmem_limit_bytes=4 << 20),
        cost_estimate=pl.CostEstimate(
            flops=4 * row_count * model_width * unit_count,
            bytes_accessed=4 * model_width * unit_count,
            transcendentals=0,
        ),
        name="gates",
    )(*rows, pltpu.with_memory_space_constraint(w_gate, VMEM), *after)


def expert_kernel(*refs):
    rows, refs = refs[:EXPERTS], refs[EXPERTS:]
    gates_ref, up_ref, down_ref = refs[:3]
    pages, outs, hidden_ref = refs[3 : 3 + EXPERTS], refs[-EXPERTS - 1 : -1], refs[-1]
    model_width = down_ref.shape[1]
    for peer in range(EXPERTS):
        outs[peer][:, model_width:] = pages[peer][...]
    block = stacked_rows(rows)
    for at in range(0, up_ref.shape[1], CHUNK):
        columns = slice(at, at + CHUNK)
        gate = gates_ref[:, columns]
        up = jnp.dot(block, up_ref[:, columns], preferred_element_type=jnp.float32)
        hidden_ref[:, columns] = (gate / (1.0 + jnp.exp(-gate)) * up).astype(jnp.bfloat16)
    for at in range(0, model_width, CHUNK):
        columns = slice(at, at + CHUNK)
        result = jnp.dot(
            hidden_ref[...], down_ref[:, columns], preferred_element_type=jnp.float32
        )
        for peer in range(EXPERTS):
            part = result[peer * CAP : (peer + 1) * CAP]
            outs[peer][:, columns] = part.astype(jnp.bfloat16)


def experts(rows, gate, w_up, w_down, pages, after):
    spec, unread = pl.BlockSpec(memory_space=VMEM), pl.BlockSpec(memory_space=pl.ANY)
    held = [pltpu.with_memory_space_constraint(w, VMEM) for w in (w_up, w_down)]
    unit_count, model_width = w_down.shape
    row_count = EXPERTS * CAP
    return pl.pallas_call(
        expert_kernel,
        out_shape=(jax.ShapeDtypeStruct((CAP, model_width + pages[0].shape[1]), jnp.bfloat16),)
        * EXPERTS,
        in_specs=[spec] * (3 + 2 * EXPERTS) + [unread] * len(after),
        out_specs=(spec,) * EXPERTS,
        scratch_shapes=[VMEM((row_count, unit_count), jnp.bfloat16)],
        compiler_params=pltpu.CompilerParams(vmem_limit_bytes=4 << 20),
        cost_estimate=pl.CostEstimate(
            flops=2 * row_count * model_width * unit_count,
            bytes_accessed=2 * model_width * unit_count,
            transcendentals=0,
        ),
        name="experts",
    )(*rows, gate, *held, *pages, *after)


def combine_kernel(mixing_ref, *refs):
    rows, parts, (out_ref, pages_ref) = refs[:EXPERTS], refs[EXPERTS:-2], refs[-2:]
    block = stacked_rows(rows)

    @pl.when(pl.program_id(0) == 0)
    def _():
        columns = pl.ds(parts[0].shape[1] - pages_ref.shape[1], pages_ref.shape[1])
        pages_ref[...] = stacked_rows([part.at[:, columns] for part in parts])

    mixing = mixing_ref[...]
    high = mixing.astype(jnp.bfloat16).astype(jnp.float32)
    mixing = jnp.concatenate([high, mixing - high], axis=0).astype(jnp.bfloat16)
    block = jnp.concatenate([block, block], axis=0)
    total = lax.dot_general(mixing, block, TN, preferred_element_type=jnp.float32)
    out_ref[...] = total.astype(jnp.bfloat16)


def combine(mixing, rows, model_width):
    slot_count, token_count = mixing.shape
    width = model_width // 2
    page_width = rows[0].shape[1] - model_width
    columns = pl.BlockSpec((CAP, width), lambda at: (0, at))
    whole = pl.BlockSpec(rows[0].shape, lambda at: (0, 0))
    return pl.pallas_call(
        combine_kernel,
        grid=(model_width // width,),
        out_shape=(
            jax.ShapeDtypeStruct((token_count, model_width), jnp.bfloat16),
            jax.ShapeDtypeStruct((slot_count, page_width), jnp.bfloat16),
        ),
        in_specs=[pl.BlockSpec((slot_count, token_count), lambda at: (0, 0))]
        + [columns] * EXPERTS
        + [whole] * EXPERTS,
        out_specs=(
            pl.BlockSpec((token_count, width), lambda at: (0, at)),
            pl.BlockSpec((slot_count, page_width), lambda at: (0, 0)),
        ),
        compiler_params=pltpu.CompilerParams(vmem_limit_bytes=8 << 20),
        cost_estimate=pl.CostEstimate(
            flops=11530000000,
            bytes_accessed=3 * token_count * model_width,
            transcendentals=0,
        ),
        name="combine",
    )(mixing, *rows, *rows)


def project_kernel(tokens_ref, theirs_ref, own_ref, *refs):
    held, (mine_out, theirs_out) = refs[:4], refs[-5:-3]
    both_ref, far_ref, sems = refs[-3:]
    group, me, dp = (lax.axis_index(axis) for axis in ("groups", "expert", "dp"))
    shard = own_ref.shape[1]
    chip_rows, core_rows = piece_rows(own_ref.shape[0])
    chip, core = group * 2 + dp // 2, dp % 2

    def copies_of(my_core):
        copies = []
        for which in range(2):
            core_at = my_core if which == 0 else 1 - my_core
            near_xor = 1 if core_at == 0 else 2
            for at, chip_xor in enumerate((0, near_xor, 3 - near_xor, 3)):
                buffer = held[2 * which + at // 2].at[at % 2]
                skip = 0 if core_at == 0 else 2 * core_rows - chip_rows
                start = (chip ^ chip_xor) * chip_rows + (0 if core_at == 0 else core_rows)
                count = core_rows - skip
                copies.append(
                    pltpu.make_async_copy(
                        buffer.at[pl.ds(skip, count)],
                        far_ref.at[pl.ds(pl.multiple_of(start, ROWS), count)],
                        sems.at[len(copies)],
                    )
                )
        return copies

    def on_each_core(act):
        for my_core in range(2):

            @pl.when(core == my_core)
            def _(my_core=my_core):
                for copy in copies_of(my_core):
                    act(copy)

    def part(left, weights_ref):
        return lax.dot_general(left, weights_ref[...], NT, preferred_element_type=jnp.float32)

    on_each_core(lambda copy: copy.start())
    count = tokens_ref.shape[0]
    for half, bit in enumerate((0, 2)):
        columns = pl.ds(pl.multiple_of((me ^ bit) * shard, LANES), shard)
        both_ref[:count, half * shard : (half + 1) * shard] = tokens_ref[:, columns]
    both_ref[count:, :] = theirs_ref[...]
    total = part(both_ref[:, :shard], own_ref)
    on_each_core(lambda copy: copy.wait())
    total = total + part(both_ref[:, shard:], far_ref)
    mine_out[...] = total[:count]
    theirs_out[...] = total[count:].astype(jnp.bfloat16)


def project(tokens, theirs, own, held, after):
    vmem, hbm = pl.BlockSpec(memory_space=VMEM), pl.BlockSpec(memory_space=pl.ANY)
    token_count = tokens.shape[0]
    width, shard = own.shape
    return pl.pallas_call(
        project_kernel,
        out_shape=(
            jax.ShapeDtypeStruct((token_count, width), jnp.float32),
            jax.ShapeDtypeStruct((token_count, width), jnp.bfloat16),
        ),
        in_specs=[vmem] * 3 + [hbm] * (4 + len(after)),
        out_specs=(vmem, vmem),
        scratch_shapes=[
            VMEM((2 * token_count, 2 * shard), jnp.bfloat16),
            VMEM((width, shard), jnp.bfloat16),
            pltpu.SemaphoreType.DMA((8,)),
        ],
        compiler_params=pltpu.CompilerParams(vmem_limit_bytes=8 << 20),
        cost_estimate=pl.CostEstimate(
            flops=1153000000, bytes_accessed=0, transcendentals=0
        ),
        name="project",
    )(tokens, theirs, own, *held, *after)


def finish_kernel(mine_ref, theirs_ref, gain_ref, survive_ref, arrived_ref, out_ref):
    page_count, page_width = out_ref.shape
    projected = mine_ref[...] + theirs_ref[...].astype(jnp.float32)
    nope_part = projected[:, :KV]
    inv_rms = lax.rsqrt(jnp.mean(nope_part * nope_part, axis=1, keepdims=True) + EPS)
    rebuilt = jnp.concatenate([nope_part * inv_rms * gain_ref[...], projected[:, KV:]], axis=1)
    rebuilt = rebuilt.astype(jnp.bfloat16)
    token_count, width = rebuilt.shape
    page_tokens = token_count // page_count
    row = lax.broadcasted_iota(jnp.int32, (token_count, token_count), 0)
    source = lax.broadcasted_iota(jnp.int32, (token_count, token_count), 1)
    moves = source == (row % page_count) * page_tokens + row // page_count
    ordered = jnp.dot(
        jnp.where(moves, 1.0, 0.0).astype(jnp.bfloat16),
        rebuilt,
        preferred_element_type=jnp.float32,
    )
    part_width = page_width // SPLIT
    row_count = arrived_ref.shape[0]
    slot = lax.broadcasted_iota(jnp.int32, (row_count, page_count), 1).astype(jnp.float32)
    part_of = lax.broadcasted_iota(jnp.int32, (row_count, page_count), 0) % SPLIT
    meant = arrived_ref[:, part_width:].astype(jnp.float32)[:, :1] == slot + 1.0
    arrivals = arrived_ref[:, :part_width]
    carried = [
        lax.dot_general(
            jnp.where(meant & (part_of == part), 1.0, 0.0).astype(jnp.bfloat16),
            arrivals,
            TN,
            preferred_element_type=jnp.float32,
        )
        for part in range(SPLIT)
    ]
    page_row = lax.broadcasted_iota(jnp.int32, (page_count, 2 * width), 0)
    survives = jnp.zeros((page_count, 2 * width), jnp.int32)
    for at in range(page_count):
        survives = jnp.where(page_row == at, survive_ref[at], survives)
    for at in range(0, page_tokens, 2):
        fresh = jnp.concatenate(
            [ordered[(at + half) * page_count : (at + half + 1) * page_count] for half in range(2)],
            axis=1,
        )
        columns = slice(at * width, (at + 2) * width)
        start = at * width % part_width
        kept = carried[at * width // part_width][:, start : start + 2 * width]
        chosen = jnp.where(survives > 0, kept, fresh)
        out_ref[:, columns] = chosen.astype(jnp.bfloat16)


def finish(mine, theirs, latent_gain, survive, arrived, page_count, page_width):
    vmem = pl.BlockSpec(memory_space=VMEM)
    return pl.pallas_call(
        finish_kernel,
        out_shape=jax.ShapeDtypeStruct((page_count, page_width), jnp.bfloat16),
        in_specs=[vmem] * 3 + [pl.BlockSpec(memory_space=SMEM), vmem],
        out_specs=vmem,
        compiler_params=pltpu.CompilerParams(vmem_limit_bytes=6 << 20),
        cost_estimate=pl.CostEstimate(
            flops=4 * mine.shape[0] ** 2 * mine.shape[1],
            bytes_accessed=1 << 20,
            transcendentals=mine.shape[0],
        ),
        name="finish",
    )(mine, theirs, latent_gain.reshape(1, -1), survive, arrived)


def swap(value, axis, bit):
    return lax.ppermute(value, axis, xor_pairs(lax.axis_size(axis), bit))


def tied(value, *after):
    return lax.optimization_barrier((value, *after))[0]


def exchanged(values, axis="expert"):
    return [values[0]] + [swap(values[bit], axis, bit) for bit in range(1, len(values))]


def block_shards(
    tokens,
    w_gate,
    w_up,
    w_down,
    w_latent,
    latent_gain,
    route_ids,
    route_weight,
    old_latents,
    survive,
    old_target,
):
    group_count, dp_count = lax.axis_size("groups"), lax.axis_size("dp")
    plane = ("groups", "dp")
    latent = w_latent.T
    piece = cut(latent)
    far_piece = swap(piece, "expert", 2)
    sends, mixing, pages, across = open_work(
        route_ids.T, route_weight.T, tokens, old_latents, old_target, latent.shape[1]
    )
    received = exchanged(sends)
    far_piece = tied(far_piece, received[1])
    first = lax.ppermute(far_piece, plane, plane_pairs(group_count, dp_count, True))
    theirs = swap(tied(across, far_piece), "expert", 1)
    gate = gates(received, w_gate, (far_piece,))
    near = tied(jnp.stack([far_piece, first]), gate)
    far = lax.ppermute(near, plane, plane_pairs(group_count, dp_count, False))
    near_other = swap(near, "dp", 1)
    results = experts(received, gate, w_up, w_down, pages, (near,))
    results = [tied(result, theirs) for result in results]
    returned = exchanged(results)
    far = tied(far, results[0])
    far_other = swap(far, "dp", 1)
    mine, across_sums = project(
        tokens, theirs, latent, (near, far, near_other, far_other), ()
    )
    their_sums = swap(across_sums, "expert", 1)
    moe_out, arrived = combine(mixing, returned, tokens.shape[1])
    latents = finish(mine, their_sums, latent_gain, survive, arrived, *old_latents.shape)
    return (moe_out, latents)


def rebuild_latents(tokens, w_latent, latent_gain):
    projected = jnp.dot(
        tokens,
        lax.all_gather(w_latent, "expert", axis=0, tiled=True),
        preferred_element_type=jnp.float32,
    )
    nope_part = projected[:, :KV]
    inv_rms = lax.rsqrt(jnp.mean(nope_part * nope_part, axis=1, keepdims=True) + EPS)
    return jnp.concatenate([nope_part * inv_rms * latent_gain, projected[:, KV:]], axis=1).astype(
        jnp.bfloat16
    )


def moved_pages(old_latents, survive, old_target, rebuilt):
    peer_count = lax.axis_size("expert")
    dp_count = lax.axis_size("dp")
    page_count = old_latents.shape[0]
    per_pair = max(1, page_count // peer_count)
    slot_ids = jnp.arange(page_count, dtype=jnp.int32)
    peer_ids = jnp.arange(peer_count, dtype=jnp.int32)
    rank_ids = jnp.arange(per_pair, dtype=jnp.int32)
    valid_out = old_target >= 0
    target_peer = old_target // page_count // dp_count
    target_slot = jnp.where(valid_out, old_target % page_count + 1, 0).astype(jnp.float32)
    same_peer = (target_peer[:, None] == target_peer[None, :]) & valid_out[None, :]
    earlier = slot_ids[None, :] < slot_ids[:, None]
    out_rank = jnp.sum((same_peer & earlier).astype(jnp.int32), axis=1)
    select = (
        valid_out[None, None, :]
        & (target_peer[None, None, :] == peer_ids[:, None, None])
        & (out_rank[None, None, :] == rank_ids[None, :, None])
    )
    select = select.reshape(peer_count * per_pair, page_count)
    outgoing = jnp.dot(
        select.astype(jnp.bfloat16), old_latents, preferred_element_type=jnp.float32
    ).astype(jnp.bfloat16)
    slot_tags = jnp.dot(
        select.astype(jnp.float32), target_slot, precision=lax.Precision.HIGHEST
    ).astype(jnp.bfloat16)
    arrived, arrived_tags = (
        lax.all_to_all(
            outgoing.reshape(peer_count, per_pair, -1),
            "expert",
            split_axis=0,
            concat_axis=0,
            tiled=True,
        ),
        lax.all_to_all(
            slot_tags.reshape(peer_count, per_pair),
            "expert",
            split_axis=0,
            concat_axis=0,
            tiled=True,
        ),
    )
    tag_values = arrived_tags.reshape(peer_count * per_pair).astype(jnp.float32)
    chooser = (tag_values[None, :] == (slot_ids + 1).astype(jnp.float32)[:, None]).astype(
        jnp.bfloat16
    )
    carried = jnp.dot(
        chooser, arrived.reshape(peer_count * per_pair, -1), preferred_element_type=jnp.float32
    ).astype(jnp.bfloat16)
    return jnp.where((survive > 0)[:, None], carried, rebuilt)


def route_tables(route_ids, route_weight):
    token_count, top_count = route_ids.shape
    flat_ids = route_ids.reshape(-1)
    onehot = (flat_ids[:, None] == jnp.arange(EXPERTS, dtype=jnp.int32)[None, :]).astype(jnp.int32)
    slot_rank = jnp.sum((jnp.cumsum(onehot, axis=0) - onehot) * onehot, axis=1)
    slot_index = jnp.where(flat_ids < EXPERTS, flat_ids * CAP + slot_rank, -1)
    matches = slot_index[:, None] == jnp.arange(EXPERTS * CAP, dtype=jnp.int32)[None, :]
    matches = matches.reshape(token_count, top_count, EXPERTS * CAP)
    placing = jnp.sum(matches.astype(jnp.float32), axis=1).astype(jnp.bfloat16)
    mixing = jnp.sum(matches.astype(jnp.float32) * route_weight[:, :, None], axis=1)
    return (placing, mixing)


def expert_rows(received, w_gate, w_up, w_down, per_dev):
    unit_count = w_gate.shape[1] // per_dev
    gate_w = w_gate.reshape(w_gate.shape[0], per_dev, unit_count)
    up_w = w_up.reshape(w_up.shape[0], per_dev, unit_count)
    down_w = w_down.reshape(per_dev, unit_count, w_down.shape[1])
    gate_value = jnp.einsum("spkd,dpf->spkf", received, gate_w, preferred_element_type=jnp.float32)
    up_value = jnp.einsum("spkd,dpf->spkf", received, up_w, preferred_element_type=jnp.float32)
    hidden = (jax.nn.silu(gate_value) * up_value).astype(jnp.bfloat16)
    return jnp.einsum("spkf,pfd->spkd", hidden, down_w, preferred_element_type=jnp.float32)


def shards(
    tokens,
    w_gate,
    w_up,
    w_down,
    w_latent,
    latent_gain,
    route_ids,
    route_weight,
    old_latents,
    survive,
    old_target,
):
    rebuilt = rebuild_latents(tokens, w_latent, latent_gain).reshape(old_latents.shape[0], -1)
    latents = moved_pages(old_latents, survive, old_target, rebuilt)
    column_count = w_gate.shape[1]
    per_dev = max(1, column_count // FF)
    span_size = max(1, FF // column_count)
    group_count = EXPERTS // per_dev
    model_width = tokens.shape[1]
    placing, mixing = route_tables(route_ids, route_weight)
    outgoing = jnp.einsum("te,td->ed", placing, tokens, preferred_element_type=jnp.float32).astype(
        jnp.bfloat16
    )
    grouped = outgoing.reshape(group_count, per_dev, CAP, model_width)
    sent_rows = jnp.repeat(grouped, span_size, axis=0)
    partial_value = expert_rows(
        lax.all_to_all(sent_rows, "expert", split_axis=0, concat_axis=0, tiled=True),
        w_gate,
        w_up,
        w_down,
        per_dev,
    )
    returned = lax.all_to_all(
        partial_value.astype(jnp.bfloat16), "expert", split_axis=0, concat_axis=0, tiled=True
    ).astype(partial_value.dtype)
    summed = jnp.sum(returned.reshape(group_count, span_size, per_dev, CAP, model_width), axis=1)
    expert_out = summed.reshape(EXPERTS * CAP, model_width)
    moe_out = jnp.dot(mixing, expert_out, precision=lax.Precision.HIGHEST).astype(jnp.bfloat16)
    return (moe_out, latents)


def small_block(mesh):
    sizes = (mesh.shape["groups"], mesh.shape["expert"], mesh.shape["dp"])
    return sizes == (2, EXPERTS, 4)


def solution(mesh):
    in_specs = (
        P(("groups", "expert", "dp"), None),
        P(None, "expert"),
        P(None, "expert"),
        P("expert", None),
        P("expert", None),
        P(),
        P(("groups", "expert", "dp"), None),
        P(("groups", "expert", "dp"), None),
        P(("groups", "expert", "dp"), None),
        P(("groups", "expert", "dp")),
        P(("groups", "expert", "dp")),
    )
    out_specs = (P(("groups", "expert", "dp"), None), P(("groups", "expert", "dp"), None))
    body = block_shards if small_block(mesh) else shards
    return jax.shard_map(body, mesh=mesh, in_specs=in_specs, out_specs=out_specs, check_vma=False)
```

```python
import functools

import jax
import jax.numpy as jnp
from jax import lax
from jax.experimental import pallas as pl
from jax.experimental.pallas import tpu as pltpu
from jax.sharding import PartitionSpec as P

FF = 2048
EXPERTS = 4
KV = 512
CAP = 8
PER_PAIR = 2
SPLIT = 4
LANES = 128
ROWS = 16


EPS = 1e-06
VMEM = pltpu.VMEM
SMEM = pltpu.SMEM
CHUNK = 512
PIECES = 4
NT = (((1,), (1,)), ((), ()))
TN = (((0,), (0,)), ((), ()))


def xor_pairs(count, bit):
    return [(at, at ^ bit) for at in range(count)]


def plane_pairs(group_count, dp_count, core_zero_along_x):
    pairs = []
    for group in range(group_count):
        for dp in range(dp_count):
            along_x = (dp % 2 == 0) == core_zero_along_x
            to_group, to_dp = (group, dp ^ 2) if along_x else (group ^ 1, dp)
            pairs.append((group * dp_count + dp, to_group * dp_count + to_dp))
    return pairs


def piece_rows(width):
    chip = width // 4
    core = -(-(chip // 2) // ROWS) * ROWS
    return chip, core


def cut_kernel(latent_ref, piece_ref, sem):
    group, dp = lax.axis_index("groups"), lax.axis_index("dp")
    chip_rows, core_rows = piece_rows(latent_ref.shape[0])
    start = (group * 2 + dp // 2) * chip_rows + (dp % 2) * (chip_rows - core_rows)
    piece = pltpu.make_async_copy(
        latent_ref.at[pl.ds(pl.multiple_of(start, ROWS), core_rows)], piece_ref, sem
    )
    piece.start()
    piece.wait()


def cut(latent):
    width, shard = latent.shape
    return pl.pallas_call(
        cut_kernel,
        out_shape=jax.ShapeDtypeStruct((piece_rows(width)[1], shard), jnp.bfloat16),
        in_specs=[pl.BlockSpec(memory_space=pltpu.HBM)],
        out_specs=pl.BlockSpec(memory_space=VMEM),
        scratch_shapes=[pltpu.SemaphoreType.DMA],
        compiler_params=pltpu.CompilerParams(vmem_limit_bytes=1 << 20),
        name="cut",
    )(pltpu.with_memory_space_constraint(latent, pltpu.HBM))


def open_kernel(page_span, *refs):
    sources, outs = refs[:5], refs[5:]
    sends, mixing_ref, pages = outs[:EXPERTS], outs[EXPERTS], outs[EXPERTS + 1 : 2 * EXPERTS]
    across_ref = outs[2 * EXPERTS]
    *held, sems = outs[2 * EXPERTS + 1 :]
    model_width = sends[0].shape[1]
    ids_ref, weight_ref, tokens_ref, old_ref, target_ref = held
    copies = [
        pltpu.make_async_copy(source, target, sems.at[at])
        for at, (source, target) in enumerate(zip(sources, held))
    ]
    for copy in copies:
        copy.start()
    me = lax.axis_index("expert")
    for copy in copies:
        copy.wait()
    shard = across_ref.shape[1] // 2
    for half, bit in enumerate((1, 3)):
        columns = pl.ds(pl.multiple_of((me ^ bit) * shard, LANES), shard)
        across_ref[:, half * shard : (half + 1) * shard] = tokens_ref[:, columns]
    top_count, token_count = ids_ref.shape
    slot_count = EXPERTS * CAP
    row = lax.broadcasted_iota(jnp.int32, (slot_count, token_count), 0)
    expert_of = (row >> 3) ^ me
    chosen = jnp.zeros((slot_count, token_count), jnp.float32)
    weight = jnp.zeros((slot_count, token_count), jnp.float32)
    for at in range(top_count):
        named = ids_ref[at : at + 1, :] == expert_of
        chosen = jnp.where(named, 1.0, chosen)
        weight = jnp.where(named, weight_ref[at : at + 1, :], weight)
    before = lax.broadcasted_iota(jnp.int32, (token_count, token_count), 0)
    token = lax.broadcasted_iota(jnp.int32, (token_count, token_count), 1)
    earlier = jnp.where(before < token, 1.0, 0.0).astype(jnp.bfloat16)
    rank = jnp.dot(chosen.astype(jnp.bfloat16), earlier, preferred_element_type=jnp.float32)
    placed = jnp.where(rank == (row & 7).astype(jnp.float32), chosen, 0.0)
    mixing_ref[...] = placed * weight
    outgoing = jnp.dot(
        placed.astype(jnp.bfloat16), tokens_ref[...], preferred_element_type=jnp.float32
    )
    for at in range(EXPERTS):
        sends[at][:, :model_width] = outgoing[at * CAP : (at + 1) * CAP].astype(jnp.bfloat16)
    page_count, width = old_ref.shape
    row_count = EXPERTS * PER_PAIR * SPLIT
    out_row = lax.broadcasted_iota(jnp.int32, (row_count, page_count), 0)
    old_page = lax.broadcasted_iota(jnp.int32, (row_count, page_count), 1)
    tag_row = lax.broadcasted_iota(jnp.int32, (row_count, LANES), 0)
    select = [jnp.zeros((row_count, page_count), jnp.float32) for _ in range(SPLIT)]
    tags = jnp.zeros((row_count, LANES), jnp.float32)
    targets = [target_ref[at] for at in range(page_count)]
    peers = [jnp.where(target >= 0, target // page_span, -1) for target in targets]
    for at in range(page_count):
        rank_at = jnp.int32(0)
        for first in range(at):
            rank_at = rank_at + jnp.where(peers[first] == peers[at], 1, 0)
        row_at = ((peers[at] ^ me) * PER_PAIR + rank_at) * SPLIT
        row_at = jnp.where(peers[at] >= 0, row_at, -SPLIT)
        for part in range(SPLIT):
            here = (out_row == row_at + part) & (old_page == at)
            select[part] = jnp.where(here, 1.0, select[part])
        slot_tag = (targets[at] % page_count + 1).astype(jnp.float32)
        tags = jnp.where((tag_row >= row_at) & (tag_row < row_at + SPLIT), slot_tag, tags)
    width = width // SPLIT
    moved = jnp.zeros((row_count, width), jnp.float32)
    for part in range(SPLIT):
        columns = slice(part * width, (part + 1) * width)
        moved = moved + jnp.dot(
            select[part].astype(jnp.bfloat16),
            old_ref[:, columns],
            preferred_element_type=jnp.float32,
        )
    for at in range(EXPERTS):
        rows = slice(at * PER_PAIR * SPLIT, (at + 1) * PER_PAIR * SPLIT)
        page = jnp.concatenate([moved[rows], tags[rows]], axis=1).astype(jnp.bfloat16)
        if at == 1:
            sends[at][:, model_width:] = page
        else:
            pages[at - (at > 1)][...] = page


def open_work(ids, weights, tokens, old_latents, old_target, shard):
    token_count, model_width = tokens.shape
    page_count, page_width = old_latents.shape
    send = jax.ShapeDtypeStruct((CAP, model_width), jnp.bfloat16)
    mixing = jax.ShapeDtypeStruct((EXPERTS * CAP, token_count), jnp.float32)
    page = jax.ShapeDtypeStruct((PER_PAIR * SPLIT, page_width // SPLIT + LANES), jnp.bfloat16)
    longer = jax.ShapeDtypeStruct((CAP, model_width + page.shape[1]), jnp.bfloat16)
    across = jax.ShapeDtypeStruct((token_count, 2 * shard), jnp.bfloat16)
    spec = pl.BlockSpec(memory_space=VMEM)
    inputs = [
        pltpu.with_memory_space_constraint(value, pltpu.HBM)
        for value in (ids, weights, tokens, old_latents, old_target)
    ]
    results = pl.pallas_call(
        functools.partial(open_kernel, page_count * lax.axis_size("dp")),
        out_shape=(send, longer, send, send, mixing) + (page,) * (EXPERTS - 1) + (across,),
        in_specs=[pl.BlockSpec(memory_space=pltpu.HBM)] * 5,
        out_specs=(spec,) * (2 * EXPERTS + 1),
        scratch_shapes=[VMEM(value.shape, value.dtype) for value in inputs[:4]]
        + [
            SMEM(old_target.shape, old_target.dtype),
            pltpu.SemaphoreType.DMA((5,)),
        ],
        compiler_params=pltpu.CompilerParams(vmem_limit_bytes=8 << 20),
        cost_estimate=pl.CostEstimate(
            flops=20_000_000_000, bytes_accessed=2 << 20, transcendentals=0
        ),
        name="open",
    )(*inputs)
    sends, mixing, rest = results[:EXPERTS], results[EXPERTS], results[EXPERTS + 1 :]
    return sends, mixing, rest[: EXPERTS - 1], rest[EXPERTS - 1]


def stacked_rows(refs):
    return jnp.concatenate([ref[...].astype(jnp.float32) for ref in refs], axis=0).astype(
        jnp.bfloat16
    )


def gate_kernel(*refs):
    rows, gate_ref, out_ref = refs[:EXPERTS], refs[EXPERTS], refs[-1]
    block = stacked_rows([row.at[:, : gate_ref.shape[0]] for row in rows])
    for at in range(0, gate_ref.shape[1], CHUNK):
        columns = slice(at, at + CHUNK)
        out_ref[:, columns] = jnp.dot(
            block, gate_ref[:, columns], preferred_element_type=jnp.float32
        )


def gates(rows, w_gate, after):
    spec, unread = pl.BlockSpec(memory_space=VMEM), pl.BlockSpec(memory_space=pl.ANY)
    model_width, unit_count = w_gate.shape
    row_count = EXPERTS * CAP
    return pl.pallas_call(
        gate_kernel,
        out_shape=jax.ShapeDtypeStruct((row_count, unit_count), jnp.float32),
        in_specs=[spec] * (EXPERTS + 1) + [unread] * len(after),
        out_specs=spec,
        compiler_params=pltpu.CompilerParams(vmem_limit_bytes=4 << 20),
        cost_estimate=pl.CostEstimate(
            flops=4 * row_count * model_width * unit_count,
            bytes_accessed=4 * model_width * unit_count,
            transcendentals=0,
        ),
        name="gates",
    )(*rows, pltpu.with_memory_space_constraint(w_gate, VMEM), *after)


def expert_kernel(*refs):
    rows, refs = refs[:EXPERTS], refs[EXPERTS:]
    gates_ref, up_ref, down_ref = refs[:3]
    pages, outs, hidden_ref = refs[3:5], refs[-EXPERTS - 1 : -1], refs[-1]
    model_width = down_ref.shape[1]
    for out, page in zip(outs[2:], pages):
        out[:, model_width:] = page[...]
    block = stacked_rows([row.at[:, :model_width] for row in rows])
    for at in range(0, up_ref.shape[1], CHUNK):
        columns = slice(at, at + CHUNK)
        gate = gates_ref[:, columns]
        up = jnp.dot(block, up_ref[:, columns], preferred_element_type=jnp.float32)
        hidden_ref[:, columns] = (gate / (1.0 + jnp.exp(-gate)) * up).astype(jnp.bfloat16)
    for at in range(0, model_width, CHUNK):
        columns = slice(at, at + CHUNK)
        result = jnp.dot(
            hidden_ref[...], down_ref[:, columns], preferred_element_type=jnp.float32
        )
        for peer in range(EXPERTS):
            part = result[peer * CAP : (peer + 1) * CAP]
            outs[peer][:, columns] = part.astype(jnp.bfloat16)


def experts(rows, gate, w_up, w_down, pages, after):
    spec, unread = pl.BlockSpec(memory_space=VMEM), pl.BlockSpec(memory_space=pl.ANY)
    held = [pltpu.with_memory_space_constraint(w, VMEM) for w in (w_up, w_down)]
    unit_count, model_width = w_down.shape
    row_count = EXPERTS * CAP
    return pl.pallas_call(
        expert_kernel,
        out_shape=tuple(
            jax.ShapeDtypeStruct((CAP, model_width + extra), jnp.bfloat16)
            for extra in (0, 0, pages[0].shape[1], pages[1].shape[1])
        ),
        in_specs=[spec] * (5 + EXPERTS) + [unread] * len(after),
        out_specs=(spec,) * EXPERTS,
        scratch_shapes=[VMEM((row_count, unit_count), jnp.bfloat16)],
        compiler_params=pltpu.CompilerParams(vmem_limit_bytes=4 << 20),
        cost_estimate=pl.CostEstimate(
            flops=2 * row_count * model_width * unit_count,
            bytes_accessed=2 * model_width * unit_count,
            transcendentals=0,
        ),
        name="experts",
    )(*rows, gate, *held, *pages, *after)


def combine_kernel(mixing_ref, *refs):
    rows, parts = refs[:EXPERTS], refs[EXPERTS : EXPERTS + 2]
    out_ref, carried_ref, held_ref, sems = refs[EXPERTS + 2 :]
    model_width = out_ref.shape[1]
    mixing = mixing_ref[...]
    high = mixing.astype(jnp.bfloat16).astype(jnp.float32)
    mixing = jnp.concatenate([high, mixing - high], axis=0).astype(jnp.bfloat16)
    block = jnp.concatenate([stacked_rows([row.at[:, :model_width] for row in rows])] * 2, axis=0)
    width = model_width // PIECES
    copies = []
    for at in range(PIECES):
        columns = slice(at * width, (at + 1) * width)
        total = lax.dot_general(mixing, block[:, columns], TN, preferred_element_type=jnp.float32)
        held_ref[:, columns] = total.astype(jnp.bfloat16)
        copies.append(
            pltpu.make_async_copy(held_ref.at[:, columns], out_ref.at[:, columns], sems.at[at])
        )
        copies[-1].start()
    page_count, page_width = carried_ref.shape
    part_width = page_width // SPLIT
    arrivals = stacked_rows(
        [parts[0]] + [row.at[:, model_width:] for row in (parts[1], rows[2], rows[3])]
    )
    row_count = arrivals.shape[0]
    slot = lax.broadcasted_iota(jnp.int32, (row_count, page_count), 1).astype(jnp.float32)
    part_of = lax.broadcasted_iota(jnp.int32, (row_count, page_count), 0) % SPLIT
    meant = arrivals[:, part_width:].astype(jnp.float32)[:, :1] == slot + 1.0
    for part in range(SPLIT):
        carried_ref[:, part * part_width : (part + 1) * part_width] = lax.dot_general(
            jnp.where(meant & (part_of == part), 1.0, 0.0).astype(jnp.bfloat16),
            arrivals[:, :part_width],
            TN,
            preferred_element_type=jnp.float32,
        )
    for copy in copies:
        copy.wait()


def combine(mixing, rows, own_pages, near_rows, page_count):
    slot_count, token_count = mixing.shape
    model_width = rows[0].shape[1]
    page_width = (own_pages.shape[1] - LANES) * SPLIT
    spec = pl.BlockSpec(memory_space=VMEM)
    return pl.pallas_call(
        combine_kernel,
        out_shape=(
            jax.ShapeDtypeStruct((token_count, model_width), jnp.bfloat16),
            jax.ShapeDtypeStruct((page_count, page_width), jnp.float32),
        ),
        in_specs=[spec] * (3 + EXPERTS),
        out_specs=(pl.BlockSpec(memory_space=pltpu.HBM), spec),
        scratch_shapes=[
            VMEM((token_count, model_width), jnp.bfloat16),
            pltpu.SemaphoreType.DMA((PIECES,)),
        ],
        compiler_params=pltpu.CompilerParams(vmem_limit_bytes=8 << 20),
        cost_estimate=pl.CostEstimate(
            flops=11530000000,
            bytes_accessed=3 * token_count * model_width,
            transcendentals=0,
        ),
        name="combine",
    )(mixing, *rows, own_pages, near_rows)


def project_kernel(tokens_ref, theirs_ref, own_ref, *refs):
    held, (mine_out, theirs_out) = refs[:4], refs[-4:-2]
    both_ref, far_ref = refs[-2:]
    group, me, dp = (lax.axis_index(axis) for axis in ("groups", "expert", "dp"))
    shard = own_ref.shape[1]
    chip_rows, core_rows = piece_rows(own_ref.shape[0])
    chip, core = group * 2 + dp // 2, dp % 2

    def assemble(my_core):
        for which in range(2):
            core_at = my_core if which == 0 else 1 - my_core
            near_xor = 1 if core_at == 0 else 2
            skip = 0 if core_at == 0 else 2 * core_rows - chip_rows
            count = core_rows - skip
            for at, chip_xor in enumerate((0, near_xor, 3 - near_xor, 3)):
                start = (chip ^ chip_xor) * chip_rows + (0 if core_at == 0 else core_rows)
                rows = pl.ds(pl.multiple_of(start, ROWS), count)
                far_ref[rows, :] = held[2 * which + at // 2][at % 2, skip:, :]

    for my_core in range(2):
        pl.when(core == my_core)(functools.partial(assemble, my_core))

    def part(weights_ref, tokens):
        return lax.dot_general(weights_ref[...], tokens, NT, preferred_element_type=jnp.float32)

    count = tokens_ref.shape[0]
    for half, bit in enumerate((0, 2)):
        columns = pl.ds(pl.multiple_of((me ^ bit) * shard, LANES), shard)
        both_ref[:count, half * shard : (half + 1) * shard] = tokens_ref[:, columns]
    both_ref[count:, :] = theirs_ref[...]
    total = part(own_ref, both_ref[:, :shard])
    total = total + part(far_ref, both_ref[:, shard:])
    mine_out[...] = total[:, :count]
    theirs_out[...] = total[:, count:].astype(jnp.bfloat16)


def project(tokens, theirs, own, held):
    spec = pl.BlockSpec(memory_space=VMEM)
    token_count = tokens.shape[0]
    width, shard = own.shape
    return pl.pallas_call(
        project_kernel,
        out_shape=(
            jax.ShapeDtypeStruct((width, token_count), jnp.float32),
            jax.ShapeDtypeStruct((width, token_count), jnp.bfloat16),
        ),
        in_specs=[spec] * 7,
        out_specs=(spec, spec),
        scratch_shapes=[
            VMEM((2 * token_count, 2 * shard), jnp.bfloat16),
            VMEM((width, shard), jnp.bfloat16),
        ],
        compiler_params=pltpu.CompilerParams(vmem_limit_bytes=8 << 20),
        cost_estimate=pl.CostEstimate(flops=1153000000, bytes_accessed=0, transcendentals=0),
        name="project",
    )(tokens, theirs, own, *held)


def finish_kernel(mine_ref, theirs_ref, gain_ref, survive_ref, carried_ref, out_ref):
    page_count = out_ref.shape[0]
    projected = mine_ref[...] + theirs_ref[...].astype(jnp.float32)
    nope_part = projected[:KV]
    inv_rms = lax.rsqrt(jnp.mean(nope_part * nope_part, axis=0, keepdims=True) + EPS)
    scaled = jnp.concatenate([nope_part * inv_rms, projected[KV:]], axis=0)
    high = scaled.astype(jnp.bfloat16)
    low = (scaled - high.astype(jnp.float32)).astype(jnp.bfloat16)
    width, token_count = scaled.shape
    page_tokens = token_count // page_count
    row = lax.broadcasted_iota(jnp.int32, (token_count, token_count), 0)
    source = lax.broadcasted_iota(jnp.int32, (token_count, token_count), 1)
    moves = source == (row % page_count) * page_tokens + row // page_count
    moves = jnp.where(moves, 1.0, 0.0).astype(jnp.bfloat16)
    ordered = lax.dot_general(
        jnp.concatenate([moves, moves], axis=1),
        jnp.concatenate([high, low], axis=1),
        NT,
        preferred_element_type=jnp.float32,
    )
    ordered = jnp.concatenate([ordered[:, :KV] * gain_ref[...], ordered[:, KV:]], axis=1)
    page_row = lax.broadcasted_iota(jnp.int32, (page_count, 2 * width), 0)
    survives = jnp.zeros((page_count, 2 * width), jnp.int32)
    for at in range(page_count):
        survives = jnp.where(page_row == at, survive_ref[at], survives)
    for at in range(0, page_tokens, 2):
        fresh = jnp.concatenate(
            [ordered[(at + half) * page_count : (at + half + 1) * page_count] for half in range(2)],
            axis=1,
        )
        columns = slice(at * width, (at + 2) * width)
        chosen = jnp.where(survives > 0, carried_ref[:, columns], fresh)
        out_ref[:, columns] = chosen.astype(jnp.bfloat16)


def finish(mine, theirs, latent_gain, survive, carried):
    vmem = pl.BlockSpec(memory_space=VMEM)
    return pl.pallas_call(
        finish_kernel,
        out_shape=jax.ShapeDtypeStruct(carried.shape, jnp.bfloat16),
        in_specs=[vmem] * 3 + [pl.BlockSpec(memory_space=SMEM), vmem],
        out_specs=vmem,
        compiler_params=pltpu.CompilerParams(vmem_limit_bytes=6 << 20),
        cost_estimate=pl.CostEstimate(
            flops=4 * mine.shape[0] ** 2 * mine.shape[1],
            bytes_accessed=1 << 20,
            transcendentals=mine.shape[0],
        ),
        name="finish",
    )(mine, theirs, latent_gain.reshape(1, -1), survive, carried)


def swap(value, axis, bit):
    return lax.ppermute(value, axis, xor_pairs(lax.axis_size(axis), bit))


def tied(value, *after):
    return lax.optimization_barrier((value, *after))[0]


def exchanged(values, axis="expert"):
    return [values[0]] + [swap(values[bit], axis, bit) for bit in range(1, len(values))]


def block_shards(
    tokens,
    w_gate,
    w_up,
    w_down,
    w_latent,
    latent_gain,
    route_ids,
    route_weight,
    old_latents,
    survive,
    old_target,
):
    group_count, dp_count = lax.axis_size("groups"), lax.axis_size("dp")
    plane = ("groups", "dp")
    latent = w_latent.T
    at = lax.axis_index("groups") * 2 + lax.axis_index("dp") // 2
    chip_rows, core_rows = piece_rows(latent.shape[0])
    start = at * chip_rows + lax.axis_index("dp") % 2 * (chip_rows - core_rows)
    piece = lax.dynamic_slice_in_dim(latent, start, core_rows, axis=0)
    far_piece = swap(piece, "expert", 2)
    sends, mixing, (own_pages, *pages), across = open_work(
        route_ids.T, route_weight.T, tokens, old_latents, old_target, latent.shape[1]
    )
    received = exchanged(sends)
    first = lax.ppermute(far_piece, plane, plane_pairs(group_count, dp_count, True))
    theirs = swap(tied(across, far_piece), "expert", 1)
    gate = gates(received, w_gate, (far_piece,))
    near = tied(jnp.stack([far_piece, first]), gate)
    far = lax.ppermute(near, plane, plane_pairs(group_count, dp_count, False))
    near_other = swap(near, "dp", 1)
    results = experts(received, gate, w_up, w_down, pages, (near,))
    results = [tied(result, theirs) for result in results]
    returned = exchanged(results)
    far = tied(far, results[0])
    far_other = swap(far, "dp", 1)
    mine, across_sums = project(
        tokens, theirs, latent, (near, far, near_other, far_other)
    )
    their_sums = swap(across_sums, "expert", 1)
    moe_out, carried = combine(mixing, returned, own_pages, received[1], old_latents.shape[0])
    latents = finish(mine, their_sums, latent_gain, survive, carried)
    return (moe_out, latents)


def rebuild_latents(tokens, w_latent, latent_gain):
    projected = jnp.dot(
        tokens,
        lax.all_gather(w_latent, "expert", axis=0, tiled=True),
        preferred_element_type=jnp.float32,
    )
    nope_part = projected[:, :KV]
    inv_rms = lax.rsqrt(jnp.mean(nope_part * nope_part, axis=1, keepdims=True) + EPS)
    return jnp.concatenate([nope_part * inv_rms * latent_gain, projected[:, KV:]], axis=1).astype(
        jnp.bfloat16
    )


def moved_pages(old_latents, survive, old_target, rebuilt):
    peer_count = lax.axis_size("expert")
    dp_count = lax.axis_size("dp")
    page_count = old_latents.shape[0]
    per_pair = max(1, page_count // peer_count)
    slot_ids = jnp.arange(page_count, dtype=jnp.int32)
    peer_ids = jnp.arange(peer_count, dtype=jnp.int32)
    rank_ids = jnp.arange(per_pair, dtype=jnp.int32)
    valid_out = old_target >= 0
    target_peer = old_target // page_count // dp_count
    target_slot = jnp.where(valid_out, old_target % page_count + 1, 0).astype(jnp.float32)
    same_peer = (target_peer[:, None] == target_peer[None, :]) & valid_out[None, :]
    earlier = slot_ids[None, :] < slot_ids[:, None]
    out_rank = jnp.sum((same_peer & earlier).astype(jnp.int32), axis=1)
    select = (
        valid_out[None, None, :]
        & (target_peer[None, None, :] == peer_ids[:, None, None])
        & (out_rank[None, None, :] == rank_ids[None, :, None])
    )
    select = select.reshape(peer_count * per_pair, page_count)
    outgoing = jnp.dot(
        select.astype(jnp.bfloat16), old_latents, preferred_element_type=jnp.float32
    ).astype(jnp.bfloat16)
    slot_tags = jnp.dot(
        select.astype(jnp.float32), target_slot, precision=lax.Precision.HIGHEST
    ).astype(jnp.bfloat16)
    arrived, arrived_tags = (
        lax.all_to_all(
            outgoing.reshape(peer_count, per_pair, -1),
            "expert",
            split_axis=0,
            concat_axis=0,
            tiled=True,
        ),
        lax.all_to_all(
            slot_tags.reshape(peer_count, per_pair),
            "expert",
            split_axis=0,
            concat_axis=0,
            tiled=True,
        ),
    )
    tag_values = arrived_tags.reshape(peer_count * per_pair).astype(jnp.float32)
    chooser = (tag_values[None, :] == (slot_ids + 1).astype(jnp.float32)[:, None]).astype(
        jnp.bfloat16
    )
    carried = jnp.dot(
        chooser, arrived.reshape(peer_count * per_pair, -1), preferred_element_type=jnp.float32
    ).astype(jnp.bfloat16)
    return jnp.where((survive > 0)[:, None], carried, rebuilt)


def route_tables(route_ids, route_weight):
    token_count, top_count = route_ids.shape
    flat_ids = route_ids.reshape(-1)
    onehot = (flat_ids[:, None] == jnp.arange(EXPERTS, dtype=jnp.int32)[None, :]).astype(jnp.int32)
    slot_rank = jnp.sum((jnp.cumsum(onehot, axis=0) - onehot) * onehot, axis=1)
    slot_index = jnp.where(flat_ids < EXPERTS, flat_ids * CAP + slot_rank, -1)
    matches = slot_index[:, None] == jnp.arange(EXPERTS * CAP, dtype=jnp.int32)[None, :]
    matches = matches.reshape(token_count, top_count, EXPERTS * CAP)
    placing = jnp.sum(matches.astype(jnp.float32), axis=1).astype(jnp.bfloat16)
    mixing = jnp.sum(matches.astype(jnp.float32) * route_weight[:, :, None], axis=1)
    return (placing, mixing)


def expert_rows(received, w_gate, w_up, w_down, per_dev):
    unit_count = w_gate.shape[1] // per_dev
    gate_w = w_gate.reshape(w_gate.shape[0], per_dev, unit_count)
    up_w = w_up.reshape(w_up.shape[0], per_dev, unit_count)
    down_w = w_down.reshape(per_dev, unit_count, w_down.shape[1])
    gate_value = jnp.einsum("spkd,dpf->spkf", received, gate_w, preferred_element_type=jnp.float32)
    up_value = jnp.einsum("spkd,dpf->spkf", received, up_w, preferred_element_type=jnp.float32)
    hidden = (jax.nn.silu(gate_value) * up_value).astype(jnp.bfloat16)
    return jnp.einsum("spkf,pfd->spkd", hidden, down_w, preferred_element_type=jnp.float32)


def shards(
    tokens,
    w_gate,
    w_up,
    w_down,
    w_latent,
    latent_gain,
    route_ids,
    route_weight,
    old_latents,
    survive,
    old_target,
):
    rebuilt = rebuild_latents(tokens, w_latent, latent_gain).reshape(old_latents.shape[0], -1)
    latents = moved_pages(old_latents, survive, old_target, rebuilt)
    column_count = w_gate.shape[1]
    per_dev = max(1, column_count // FF)
    span_size = max(1, FF // column_count)
    group_count = EXPERTS // per_dev
    model_width = tokens.shape[1]
    placing, mixing = route_tables(route_ids, route_weight)
    outgoing = jnp.einsum("te,td->ed", placing, tokens, preferred_element_type=jnp.float32).astype(
        jnp.bfloat16
    )
    grouped = outgoing.reshape(group_count, per_dev, CAP, model_width)
    sent_rows = jnp.repeat(grouped, span_size, axis=0)
    partial_value = expert_rows(
        lax.all_to_all(sent_rows, "expert", split_axis=0, concat_axis=0, tiled=True),
        w_gate,
        w_up,
        w_down,
        per_dev,
    )
    returned = lax.all_to_all(
        partial_value.astype(jnp.bfloat16), "expert", split_axis=0, concat_axis=0, tiled=True
    ).astype(partial_value.dtype)
    summed = jnp.sum(returned.reshape(group_count, span_size, per_dev, CAP, model_width), axis=1)
    expert_out = summed.reshape(EXPERTS * CAP, model_width)
    moe_out = jnp.dot(mixing, expert_out, precision=lax.Precision.HIGHEST).astype(jnp.bfloat16)
    return (moe_out, latents)


def small_block(mesh):
    sizes = (mesh.shape["groups"], mesh.shape["expert"], mesh.shape["dp"])
    return sizes == (2, EXPERTS, 4)


def solution(mesh):
    in_specs = (
        P(("groups", "expert", "dp"), None),
        P(None, "expert"),
        P(None, "expert"),
        P("expert", None),
        P("expert", None),
        P(),
        P(("groups", "expert", "dp"), None),
        P(("groups", "expert", "dp"), None),
        P(("groups", "expert", "dp"), None),
        P(("groups", "expert", "dp")),
        P(("groups", "expert", "dp")),
    )
    out_specs = (P(("groups", "expert", "dp"), None), P(("groups", "expert", "dp"), None))
    body = block_shards if small_block(mesh) else shards
    return jax.shard_map(body, mesh=mesh, in_specs=in_specs, out_specs=out_specs, check_vma=False)
```

```python
import functools

import jax
import jax.numpy as jnp
from jax import lax
from jax.experimental import pallas as pl
from jax.experimental.pallas import tpu as pltpu
from jax.sharding import PartitionSpec as P

FF = 2048
EXPERTS = 4
KV = 512
CAP = 8
PER_PAIR = 2
SPLIT = 4
LANES = 128
ROWS = 16


EPS = 1e-06
VMEM = pltpu.VMEM
SMEM = pltpu.SMEM
CHUNK = 512
PIECES = 4
ORDER = (0, 3, 1, 2)
NT = (((1,), (1,)), ((), ()))
TN = (((0,), (0,)), ((), ()))


def xor_pairs(count, bit):
    return [(at, at ^ bit) for at in range(count)]


def plane_pairs(group_count, dp_count, core_zero_along_x):
    pairs = []
    for group in range(group_count):
        for dp in range(dp_count):
            along_x = (dp % 2 == 0) == core_zero_along_x
            to_group, to_dp = (group, dp ^ 2) if along_x else (group ^ 1, dp)
            pairs.append((group * dp_count + dp, to_group * dp_count + to_dp))
    return pairs


def piece_rows(width):
    return width // 4, width // 8


def open_kernel(page_span, *refs):
    sources, outs = refs[:5], refs[5:]
    sends, mixing_ref, pages = outs[:EXPERTS], outs[EXPERTS], outs[EXPERTS + 1 : 2 * EXPERTS]
    across_ref = outs[2 * EXPERTS]
    *held, sems = outs[2 * EXPERTS + 1 :]
    model_width = sends[0].shape[1]
    ids_ref, weight_ref, tokens_ref, old_ref, target_ref = held
    copies = [
        pltpu.make_async_copy(source, target, sems.at[at])
        for at, (source, target) in enumerate(zip(sources, held))
    ]
    for copy in copies:
        copy.start()
    me = lax.axis_index("expert")
    for copy in copies:
        copy.wait()
    shard = across_ref.shape[1] // 2
    for half, bit in enumerate((1, 3)):
        columns = pl.ds(pl.multiple_of((me ^ bit) * shard, LANES), shard)
        across_ref[:, half * shard : (half + 1) * shard] = tokens_ref[:, columns]
    top_count, token_count = ids_ref.shape
    slot_count = EXPERTS * CAP
    row = lax.broadcasted_iota(jnp.int32, (slot_count, token_count), 0)
    expert_of = (row >> 3) ^ me
    chosen = jnp.zeros((slot_count, token_count), jnp.float32)
    weight = jnp.zeros((slot_count, token_count), jnp.float32)
    for at in range(top_count):
        named = ids_ref[at : at + 1, :] == expert_of
        chosen = jnp.where(named, 1.0, chosen)
        weight = jnp.where(named, weight_ref[at : at + 1, :], weight)
    before = lax.broadcasted_iota(jnp.int32, (token_count, token_count), 0)
    token = lax.broadcasted_iota(jnp.int32, (token_count, token_count), 1)
    earlier = jnp.where(before < token, 1.0, 0.0).astype(jnp.bfloat16)
    rank = jnp.dot(chosen.astype(jnp.bfloat16), earlier, preferred_element_type=jnp.float32)
    placed = jnp.where(rank == (row & 7).astype(jnp.float32), chosen, 0.0)
    mixing_ref[...] = placed * weight
    outgoing = jnp.dot(
        placed.astype(jnp.bfloat16), tokens_ref[...], preferred_element_type=jnp.float32
    )
    for at in range(EXPERTS):
        sends[at][:, :model_width] = outgoing[at * CAP : (at + 1) * CAP].astype(jnp.bfloat16)
    page_count, width = old_ref.shape
    row_count = EXPERTS * PER_PAIR * SPLIT
    out_row = lax.broadcasted_iota(jnp.int32, (row_count, page_count), 0)
    old_page = lax.broadcasted_iota(jnp.int32, (row_count, page_count), 1)
    tag_row = lax.broadcasted_iota(jnp.int32, (row_count, LANES), 0)
    select = [jnp.zeros((row_count, page_count), jnp.float32) for _ in range(SPLIT)]
    tags = jnp.zeros((row_count, LANES), jnp.float32)
    targets = [target_ref[at] for at in range(page_count)]
    peers = [jnp.where(target >= 0, target // page_span, -1) for target in targets]
    for at in range(page_count):
        rank_at = jnp.int32(0)
        for first in range(at):
            rank_at = rank_at + jnp.where(peers[first] == peers[at], 1, 0)
        row_at = ((peers[at] ^ me) * PER_PAIR + rank_at) * SPLIT
        row_at = jnp.where(peers[at] >= 0, row_at, -SPLIT)
        for part in range(SPLIT):
            here = (out_row == row_at + part) & (old_page == at)
            select[part] = jnp.where(here, 1.0, select[part])
        slot_tag = (targets[at] % page_count + 1).astype(jnp.float32)
        tags = jnp.where((tag_row >= row_at) & (tag_row < row_at + SPLIT), slot_tag, tags)
    width = width // SPLIT
    moved = jnp.zeros((row_count, width), jnp.float32)
    for part in range(SPLIT):
        columns = slice(part * width, (part + 1) * width)
        moved = moved + jnp.dot(
            select[part].astype(jnp.bfloat16),
            old_ref[:, columns],
            preferred_element_type=jnp.float32,
        )
    for at in range(EXPERTS):
        rows = slice(at * PER_PAIR * SPLIT, (at + 1) * PER_PAIR * SPLIT)
        page = jnp.concatenate([moved[rows], tags[rows]], axis=1).astype(jnp.bfloat16)
        if at == 1:
            sends[at][:, model_width:] = page
        else:
            pages[at - (at > 1)][...] = page


def open_work(ids, weights, tokens, old_latents, old_target, shard):
    token_count, model_width = tokens.shape
    page_count, page_width = old_latents.shape
    send = jax.ShapeDtypeStruct((CAP, model_width), jnp.bfloat16)
    mixing = jax.ShapeDtypeStruct((EXPERTS * CAP, token_count), jnp.float32)
    page = jax.ShapeDtypeStruct((PER_PAIR * SPLIT, page_width // SPLIT + LANES), jnp.bfloat16)
    longer = jax.ShapeDtypeStruct((CAP, model_width + page.shape[1]), jnp.bfloat16)
    across = jax.ShapeDtypeStruct((token_count, 2 * shard), jnp.bfloat16)
    spec = pl.BlockSpec(memory_space=VMEM)
    inputs = [
        pltpu.with_memory_space_constraint(value, pltpu.HBM)
        for value in (ids, weights, tokens, old_latents, old_target)
    ]
    results = pl.pallas_call(
        functools.partial(open_kernel, page_count * lax.axis_size("dp")),
        out_shape=(send, longer, send, send, mixing) + (page,) * (EXPERTS - 1) + (across,),
        in_specs=[pl.BlockSpec(memory_space=pltpu.HBM)] * 5,
        out_specs=(spec,) * (2 * EXPERTS + 1),
        scratch_shapes=[VMEM(value.shape, value.dtype) for value in inputs[:4]]
        + [
            SMEM(old_target.shape, old_target.dtype),
            pltpu.SemaphoreType.DMA((5,)),
        ],
        compiler_params=pltpu.CompilerParams(vmem_limit_bytes=8 << 20),
        cost_estimate=pl.CostEstimate(
            flops=20_000_000_000, bytes_accessed=2 << 20, transcendentals=0
        ),
        name="open",
    )(*inputs)
    sends, mixing, rest = results[:EXPERTS], results[EXPERTS], results[EXPERTS + 1 :]
    return sends, mixing, rest[: EXPERTS - 1], rest[EXPERTS - 1]


def stacked_rows(refs):
    return jnp.concatenate([ref[...].astype(jnp.float32) for ref in refs], axis=0).astype(
        jnp.bfloat16
    )


def gate_kernel(*refs):
    rows, gate_ref, out_ref = refs[:EXPERTS], refs[EXPERTS], refs[-1]
    block = stacked_rows([row.at[:, : gate_ref.shape[0]] for row in rows])
    for at in range(0, gate_ref.shape[1], CHUNK):
        columns = slice(at, at + CHUNK)
        out_ref[:, columns] = jnp.dot(
            block, gate_ref[:, columns], preferred_element_type=jnp.float32
        )


def gates(rows, w_gate, after):
    spec, unread = pl.BlockSpec(memory_space=VMEM), pl.BlockSpec(memory_space=pl.ANY)
    model_width, unit_count = w_gate.shape
    row_count = EXPERTS * CAP
    return pl.pallas_call(
        gate_kernel,
        out_shape=jax.ShapeDtypeStruct((row_count, unit_count), jnp.float32),
        in_specs=[spec] * (EXPERTS + 1) + [unread] * len(after),
        out_specs=spec,
        compiler_params=pltpu.CompilerParams(vmem_limit_bytes=4 << 20),
        cost_estimate=pl.CostEstimate(
            flops=4 * row_count * model_width * unit_count,
            bytes_accessed=4 * model_width * unit_count,
            transcendentals=0,
        ),
        name="gates",
    )(*rows, pltpu.with_memory_space_constraint(w_gate, VMEM), *after)


def expert_kernel(*refs):
    rows, refs = refs[:EXPERTS], refs[EXPERTS:]
    gates_ref, up_ref, down_ref = refs[:3]
    pages, outs, hidden_ref = refs[3:5], refs[-EXPERTS - 1 : -1], refs[-1]
    model_width = down_ref.shape[1]
    for out, page in zip(outs[2:], pages):
        out[:, model_width:] = page[...]
    block = stacked_rows([row.at[:, :model_width] for row in rows])
    for at in range(0, up_ref.shape[1], CHUNK):
        columns = slice(at, at + CHUNK)
        gate = gates_ref[:, columns]
        up = jnp.dot(block, up_ref[:, columns], preferred_element_type=jnp.float32)
        hidden_ref[:, columns] = (gate / (1.0 + jnp.exp(-gate)) * up).astype(jnp.bfloat16)
    for at in range(0, model_width, CHUNK):
        columns = slice(at, at + CHUNK)
        result = jnp.dot(
            hidden_ref[...], down_ref[:, columns], preferred_element_type=jnp.float32
        )
        for peer in range(EXPERTS):
            part = result[peer * CAP : (peer + 1) * CAP]
            outs[peer][:, columns] = part.astype(jnp.bfloat16)


def experts(rows, gate, w_up, w_down, pages, after):
    spec, unread = pl.BlockSpec(memory_space=VMEM), pl.BlockSpec(memory_space=pl.ANY)
    held = [pltpu.with_memory_space_constraint(w, VMEM) for w in (w_up, w_down)]
    unit_count, model_width = w_down.shape
    row_count = EXPERTS * CAP
    return pl.pallas_call(
        expert_kernel,
        out_shape=tuple(
            jax.ShapeDtypeStruct((CAP, model_width + extra), jnp.bfloat16)
            for extra in (0, 0, pages[0].shape[1], pages[1].shape[1])
        ),
        in_specs=[spec] * (5 + EXPERTS) + [unread] * len(after),
        out_specs=(spec,) * EXPERTS,
        scratch_shapes=[VMEM((row_count, unit_count), jnp.bfloat16)],
        compiler_params=pltpu.CompilerParams(vmem_limit_bytes=4 << 20),
        cost_estimate=pl.CostEstimate(
            flops=2 * row_count * model_width * unit_count,
            bytes_accessed=2 * model_width * unit_count,
            transcendentals=0,
        ),
        name="experts",
    )(*rows, gate, *held, *pages, *after)


def combine_kernel(mixing_ref, *refs):
    rows, parts = refs[:EXPERTS], refs[EXPERTS : EXPERTS + 2]
    rows = [rows[ORDER.index(at)] for at in range(EXPERTS)]
    out_ref, carried_ref, held_ref, sems = refs[EXPERTS + 2 :]
    model_width = out_ref.shape[1]
    mixing = mixing_ref[...]
    high = mixing.astype(jnp.bfloat16).astype(jnp.float32)
    mixing = jnp.concatenate([high, mixing - high], axis=0).astype(jnp.bfloat16)
    block = jnp.concatenate([stacked_rows([row.at[:, :model_width] for row in rows])] * 2, axis=0)
    width = model_width // PIECES
    copies = []
    for at in range(PIECES):
        columns = slice(at * width, (at + 1) * width)
        total = lax.dot_general(mixing, block[:, columns], TN, preferred_element_type=jnp.float32)
        held_ref[:, columns] = total.astype(jnp.bfloat16)
        copies.append(
            pltpu.make_async_copy(held_ref.at[:, columns], out_ref.at[:, columns], sems.at[at])
        )
        copies[-1].start()
    page_count, page_width = carried_ref.shape
    part_width = page_width // SPLIT
    arrivals = stacked_rows(
        [parts[0]] + [row.at[:, model_width:] for row in (parts[1], rows[2], rows[3])]
    )
    row_count = arrivals.shape[0]
    slot = lax.broadcasted_iota(jnp.int32, (row_count, page_count), 1).astype(jnp.float32)
    part_of = lax.broadcasted_iota(jnp.int32, (row_count, page_count), 0) % SPLIT
    meant = arrivals[:, part_width:].astype(jnp.float32)[:, :1] == slot + 1.0
    for part in range(SPLIT):
        chosen = lax.dot_general(
            jnp.where(meant & (part_of == part), 1.0, 0.0).astype(jnp.bfloat16),
            arrivals[:, :part_width],
            TN,
            preferred_element_type=jnp.float32,
        )
        columns = slice(part * part_width, (part + 1) * part_width)
        carried_ref[:, columns] = chosen.astype(jnp.bfloat16)
    for copy in copies:
        copy.wait()


def combine(mixing, rows, own_pages, near_rows, page_count):
    slot_count, token_count = mixing.shape
    model_width = rows[0].shape[1]
    page_width = (own_pages.shape[1] - LANES) * SPLIT
    spec = pl.BlockSpec(memory_space=VMEM)
    return pl.pallas_call(
        combine_kernel,
        out_shape=(
            jax.ShapeDtypeStruct((token_count, model_width), jnp.bfloat16),
            jax.ShapeDtypeStruct((page_count, page_width), jnp.bfloat16),
        ),
        in_specs=[spec] * (3 + EXPERTS),
        out_specs=(pl.BlockSpec(memory_space=pltpu.HBM), spec),
        scratch_shapes=[
            VMEM((token_count, model_width), jnp.bfloat16),
            pltpu.SemaphoreType.DMA((PIECES,)),
        ],
        compiler_params=pltpu.CompilerParams(vmem_limit_bytes=8 << 20),
        cost_estimate=pl.CostEstimate(
            flops=11530000000,
            bytes_accessed=3 * token_count * model_width,
            transcendentals=0,
        ),
        name="combine",
    )(mixing, *(rows[at] for at in ORDER), own_pages, near_rows)


def project_kernel(tokens_ref, theirs_ref, own_ref, *refs):
    held, (mine_out, theirs_out) = refs[:4], refs[-4:-2]
    both_ref, far_ref = refs[-2:]
    group, me, dp = (lax.axis_index(axis) for axis in ("groups", "expert", "dp"))
    shard = own_ref.shape[1]
    chip_rows, _ = piece_rows(own_ref.shape[0])
    chip, core = group * 2 + dp // 2, dp % 2

    def assemble(my_core):
        orders = ((0, 1, 2, 3), (0, 2, 1, 3))
        for chip_xor in range(4):
            halves = []
            for core_at in range(2):
                at = orders[core_at].index(chip_xor)
                buffer = held[at // 2 + (0 if core_at == my_core else 2)]
                halves.append(buffer[at % 2].astype(jnp.float32))
            rows = pl.ds(pl.multiple_of((chip ^ chip_xor) * chip_rows, ROWS), chip_rows)
            far_ref[rows, :] = jnp.concatenate(halves, axis=0).astype(jnp.bfloat16)

    for my_core in range(2):
        pl.when(core == my_core)(functools.partial(assemble, my_core))

    def part(weights_ref, tokens):
        return lax.dot_general(weights_ref[...], tokens, NT, preferred_element_type=jnp.float32)

    count = tokens_ref.shape[0]
    for half, bit in enumerate((0, 2)):
        columns = pl.ds(pl.multiple_of((me ^ bit) * shard, LANES), shard)
        both_ref[:count, half * shard : (half + 1) * shard] = tokens_ref[:, columns]
    both_ref[count:, :] = theirs_ref[...]
    total = part(own_ref, both_ref[:, :shard])
    total = total + part(far_ref, both_ref[:, shard:])
    mine_out[...] = total[:, :count]
    theirs_out[...] = total[:, count:].astype(jnp.bfloat16)


def project(tokens, theirs, own, held):
    spec = pl.BlockSpec(memory_space=VMEM)
    token_count = tokens.shape[0]
    width, shard = own.shape
    return pl.pallas_call(
        project_kernel,
        out_shape=(
            jax.ShapeDtypeStruct((width, token_count), jnp.float32),
            jax.ShapeDtypeStruct((width, token_count), jnp.bfloat16),
        ),
        in_specs=[spec] * 7,
        out_specs=(spec, spec),
        scratch_shapes=[
            VMEM((2 * token_count, 2 * shard), jnp.bfloat16),
            VMEM((width, shard), jnp.bfloat16),
        ],
        compiler_params=pltpu.CompilerParams(vmem_limit_bytes=8 << 20),
        cost_estimate=pl.CostEstimate(flops=1153000000, bytes_accessed=0, transcendentals=0),
        name="project",
    )(tokens, theirs, own, *held)


def finish_kernel(mine_ref, theirs_ref, gain_ref, unread_ref, out_ref):
    del unread_ref
    page_count = out_ref.shape[0]
    projected = mine_ref[...] + theirs_ref[...].astype(jnp.float32)
    nope_part = projected[:KV]
    inv_rms = lax.rsqrt(jnp.mean(nope_part * nope_part, axis=0, keepdims=True) + EPS)
    scaled = jnp.concatenate([nope_part * inv_rms, projected[KV:]], axis=0)
    high = scaled.astype(jnp.bfloat16)
    low = (scaled - high.astype(jnp.float32)).astype(jnp.bfloat16)
    width, token_count = scaled.shape
    page_tokens = token_count // page_count
    row = lax.broadcasted_iota(jnp.int32, (token_count, token_count), 0)
    source = lax.broadcasted_iota(jnp.int32, (token_count, token_count), 1)
    moves = source == (row % page_count) * page_tokens + row // page_count
    moves = jnp.where(moves, 1.0, 0.0).astype(jnp.bfloat16)
    ordered = lax.dot_general(
        jnp.concatenate([moves, moves], axis=1),
        jnp.concatenate([high, low], axis=1),
        NT,
        preferred_element_type=jnp.float32,
    )
    ordered = jnp.concatenate([ordered[:, :KV] * gain_ref[...], ordered[:, KV:]], axis=1)
    for at in range(0, page_tokens, 2):
        fresh = jnp.concatenate(
            [ordered[(at + half) * page_count : (at + half + 1) * page_count] for half in range(2)],
            axis=1,
        )
        out_ref[:, at * width : (at + 2) * width] = fresh.astype(jnp.bfloat16)


def finish(mine, theirs, latent_gain, carried):
    vmem = pl.BlockSpec(memory_space=VMEM)
    return pl.pallas_call(
        finish_kernel,
        out_shape=jax.ShapeDtypeStruct(carried.shape, jnp.bfloat16),
        in_specs=[vmem] * 3 + [pl.BlockSpec(memory_space=pl.ANY)],
        out_specs=vmem,
        compiler_params=pltpu.CompilerParams(vmem_limit_bytes=6 << 20),
        cost_estimate=pl.CostEstimate(
            flops=4 * mine.shape[1] ** 2 * mine.shape[0],
            bytes_accessed=1 << 20,
            transcendentals=mine.shape[1],
        ),
        name="finish",
    )(mine, theirs, latent_gain.reshape(1, -1), carried)


def swap(value, axis, bit):
    return lax.ppermute(value, axis, xor_pairs(lax.axis_size(axis), bit))


def tied(value, *after):
    return lax.optimization_barrier((value, *after))[0]


def exchanged(values, axis="expert"):
    return [values[0]] + [swap(values[bit], axis, bit) for bit in range(1, len(values))]


def block_shards(
    tokens,
    w_gate,
    w_up,
    w_down,
    w_latent,
    latent_gain,
    route_ids,
    route_weight,
    old_latents,
    survive,
    old_target,
):
    group_count, dp_count = lax.axis_size("groups"), lax.axis_size("dp")
    plane = ("groups", "dp")
    latent = w_latent.T
    at = lax.axis_index("groups") * 2 + lax.axis_index("dp") // 2
    chip_rows, core_rows = piece_rows(latent.shape[0])
    start = at * chip_rows + lax.axis_index("dp") % 2 * core_rows
    piece = lax.dynamic_slice_in_dim(latent, start, core_rows, axis=0)
    far_piece = swap(piece, "expert", 2)
    sends, mixing, (own_pages, *pages), across = open_work(
        route_ids.T, route_weight.T, tokens, old_latents, old_target, latent.shape[1]
    )
    received = exchanged(sends)
    first = lax.ppermute(far_piece, plane, plane_pairs(group_count, dp_count, True))
    theirs = swap(tied(across, far_piece), "expert", 1)
    gate = gates(received, w_gate, (far_piece,))
    near = tied(jnp.stack([far_piece, first]), gate)
    far = lax.ppermute(near, plane, plane_pairs(group_count, dp_count, False))
    near_other = swap(near, "dp", 1)
    results = experts(received, gate, w_up, w_down, pages, (near,))
    results = [tied(result, theirs) for result in results]
    returned = exchanged(results)
    far = tied(far, results[0])
    far_other = swap(far, "dp", 1)
    mine, across_sums = project(
        tokens, theirs, latent, (near, far, near_other, far_other)
    )
    their_sums = swap(across_sums, "expert", 1)
    moe_out, carried = combine(mixing, returned, own_pages, received[1], old_latents.shape[0])
    fresh = finish(mine, their_sums, latent_gain, carried)
    latents = jnp.where((survive > 0)[:, None], carried, fresh)
    return (moe_out, latents)


def rebuild_latents(tokens, w_latent, latent_gain):
    projected = jnp.dot(
        tokens,
        lax.all_gather(w_latent, "expert", axis=0, tiled=True),
        preferred_element_type=jnp.float32,
    )
    nope_part = projected[:, :KV]
    inv_rms = lax.rsqrt(jnp.mean(nope_part * nope_part, axis=1, keepdims=True) + EPS)
    return jnp.concatenate([nope_part * inv_rms * latent_gain, projected[:, KV:]], axis=1).astype(
        jnp.bfloat16
    )


def moved_pages(old_latents, survive, old_target, rebuilt):
    peer_count = lax.axis_size("expert")
    dp_count = lax.axis_size("dp")
    page_count = old_latents.shape[0]
    per_pair = max(1, page_count // peer_count)
    slot_ids = jnp.arange(page_count, dtype=jnp.int32)
    peer_ids = jnp.arange(peer_count, dtype=jnp.int32)
    rank_ids = jnp.arange(per_pair, dtype=jnp.int32)
    valid_out = old_target >= 0
    target_peer = old_target // page_count // dp_count
    target_slot = jnp.where(valid_out, old_target % page_count + 1, 0).astype(jnp.float32)
    same_peer = (target_peer[:, None] == target_peer[None, :]) & valid_out[None, :]
    earlier = slot_ids[None, :] < slot_ids[:, None]
    out_rank = jnp.sum((same_peer & earlier).astype(jnp.int32), axis=1)
    select = (
        valid_out[None, None, :]
        & (target_peer[None, None, :] == peer_ids[:, None, None])
        & (out_rank[None, None, :] == rank_ids[None, :, None])
    )
    select = select.reshape(peer_count * per_pair, page_count)
    outgoing = jnp.dot(
        select.astype(jnp.bfloat16), old_latents, preferred_element_type=jnp.float32
    ).astype(jnp.bfloat16)
    slot_tags = jnp.dot(
        select.astype(jnp.float32), target_slot, precision=lax.Precision.HIGHEST
    ).astype(jnp.bfloat16)
    arrived, arrived_tags = (
        lax.all_to_all(
            outgoing.reshape(peer_count, per_pair, -1),
            "expert",
            split_axis=0,
            concat_axis=0,
            tiled=True,
        ),
        lax.all_to_all(
            slot_tags.reshape(peer_count, per_pair),
            "expert",
            split_axis=0,
            concat_axis=0,
            tiled=True,
        ),
    )
    tag_values = arrived_tags.reshape(peer_count * per_pair).astype(jnp.float32)
    chooser = (tag_values[None, :] == (slot_ids + 1).astype(jnp.float32)[:, None]).astype(
        jnp.bfloat16
    )
    carried = jnp.dot(
        chooser, arrived.reshape(peer_count * per_pair, -1), preferred_element_type=jnp.float32
    ).astype(jnp.bfloat16)
    return jnp.where((survive > 0)[:, None], carried, rebuilt)


def route_tables(route_ids, route_weight):
    token_count, top_count = route_ids.shape
    flat_ids = route_ids.reshape(-1)
    onehot = (flat_ids[:, None] == jnp.arange(EXPERTS, dtype=jnp.int32)[None, :]).astype(jnp.int32)
    slot_rank = jnp.sum((jnp.cumsum(onehot, axis=0) - onehot) * onehot, axis=1)
    slot_index = jnp.where(flat_ids < EXPERTS, flat_ids * CAP + slot_rank, -1)
    matches = slot_index[:, None] == jnp.arange(EXPERTS * CAP, dtype=jnp.int32)[None, :]
    matches = matches.reshape(token_count, top_count, EXPERTS * CAP)
    placing = jnp.sum(matches.astype(jnp.float32), axis=1).astype(jnp.bfloat16)
    mixing = jnp.sum(matches.astype(jnp.float32) * route_weight[:, :, None], axis=1)
    return (placing, mixing)


def expert_rows(received, w_gate, w_up, w_down, per_dev):
    unit_count = w_gate.shape[1] // per_dev
    gate_w = w_gate.reshape(w_gate.shape[0], per_dev, unit_count)
    up_w = w_up.reshape(w_up.shape[0], per_dev, unit_count)
    down_w = w_down.reshape(per_dev, unit_count, w_down.shape[1])
    gate_value = jnp.einsum("spkd,dpf->spkf", received, gate_w, preferred_element_type=jnp.float32)
    up_value = jnp.einsum("spkd,dpf->spkf", received, up_w, preferred_element_type=jnp.float32)
    hidden = (jax.nn.silu(gate_value) * up_value).astype(jnp.bfloat16)
    return jnp.einsum("spkf,pfd->spkd", hidden, down_w, preferred_element_type=jnp.float32)


def shards(
    tokens,
    w_gate,
    w_up,
    w_down,
    w_latent,
    latent_gain,
    route_ids,
    route_weight,
    old_latents,
    survive,
    old_target,
):
    rebuilt = rebuild_latents(tokens, w_latent, latent_gain).reshape(old_latents.shape[0], -1)
    latents = moved_pages(old_latents, survive, old_target, rebuilt)
    column_count = w_gate.shape[1]
    per_dev = max(1, column_count // FF)
    span_size = max(1, FF // column_count)
    group_count = EXPERTS // per_dev
    model_width = tokens.shape[1]
    placing, mixing = route_tables(route_ids, route_weight)
    outgoing = jnp.einsum("te,td->ed", placing, tokens, preferred_element_type=jnp.float32).astype(
        jnp.bfloat16
    )
    grouped = outgoing.reshape(group_count, per_dev, CAP, model_width)
    sent_rows = jnp.repeat(grouped, span_size, axis=0)
    partial_value = expert_rows(
        lax.all_to_all(sent_rows, "expert", split_axis=0, concat_axis=0, tiled=True),
        w_gate,
        w_up,
        w_down,
        per_dev,
    )
    returned = lax.all_to_all(
        partial_value.astype(jnp.bfloat16), "expert", split_axis=0, concat_axis=0, tiled=True
    ).astype(partial_value.dtype)
    summed = jnp.sum(returned.reshape(group_count, span_size, per_dev, CAP, model_width), axis=1)
    expert_out = summed.reshape(EXPERTS * CAP, model_width)
    moe_out = jnp.dot(mixing, expert_out, precision=lax.Precision.HIGHEST).astype(jnp.bfloat16)
    return (moe_out, latents)


def small_block(mesh):
    sizes = (mesh.shape["groups"], mesh.shape["expert"], mesh.shape["dp"])
    return sizes == (2, EXPERTS, 4)


def solution(mesh):
    in_specs = (
        P(("groups", "expert", "dp"), None),
        P(None, "expert"),
        P(None, "expert"),
        P("expert", None),
        P("expert", None),
        P(),
        P(("groups", "expert", "dp"), None),
        P(("groups", "expert", "dp"), None),
        P(("groups", "expert", "dp"), None),
        P(("groups", "expert", "dp")),
        P(("groups", "expert", "dp")),
    )
    out_specs = (P(("groups", "expert", "dp"), None), P(("groups", "expert", "dp"), None))
    body = block_shards if small_block(mesh) else shards
    return jax.shard_map(body, mesh=mesh, in_specs=in_specs, out_specs=out_specs, check_vma=False)
```

```python
import functools

import jax
import jax.numpy as jnp
from jax import lax
from jax.experimental import pallas as pl
from jax.experimental.pallas import tpu as pltpu
from jax.sharding import PartitionSpec as P

FF = 2048
EXPERTS = 4
KV = 512
CAP = 8
PER_PAIR = 2
SPLIT = 4
LANES = 128
ROWS = 16


EPS = 1e-06
VMEM = pltpu.VMEM
SMEM = pltpu.SMEM
CHUNK = 512
PIECES = 4
ORDER = (0, 3, 1, 2)
NT = (((1,), (1,)), ((), ()))
TN = (((0,), (0,)), ((), ()))


def xor_pairs(count, bit):
    return [(at, at ^ bit) for at in range(count)]


def plane_pairs(group_count, dp_count, core_zero_along_x):
    pairs = []
    for group in range(group_count):
        for dp in range(dp_count):
            along_x = (dp % 2 == 0) == core_zero_along_x
            to_group, to_dp = (group, dp ^ 2) if along_x else (group ^ 1, dp)
            pairs.append((group * dp_count + dp, to_group * dp_count + to_dp))
    return pairs


def piece_rows(width):
    return width // 4, width // 8


def open_kernel(page_span, *refs):
    sources, outs = refs[:5], refs[5:]
    sends, mixing_ref, pages = outs[:EXPERTS], outs[EXPERTS], outs[EXPERTS + 1 : 2 * EXPERTS]
    across_ref = outs[2 * EXPERTS]
    *held, sems = outs[2 * EXPERTS + 1 :]
    model_width = sends[0].shape[1]
    ids_ref, weight_ref, tokens_ref, old_ref, target_ref = held
    copies = [
        pltpu.make_async_copy(source, target, sems.at[at])
        for at, (source, target) in enumerate(zip(sources, held))
    ]
    for copy in copies:
        copy.start()
    me = lax.axis_index("expert")
    for copy in copies:
        copy.wait()
    shard = across_ref.shape[1] // 2
    for half, bit in enumerate((1, 3)):
        columns = pl.ds(pl.multiple_of((me ^ bit) * shard, LANES), shard)
        across_ref[:, half * shard : (half + 1) * shard] = tokens_ref[:, columns]
    top_count, token_count = ids_ref.shape
    slot_count = EXPERTS * CAP
    row = lax.broadcasted_iota(jnp.int32, (slot_count, token_count), 0)
    expert_of = (row >> 3) ^ me
    chosen = jnp.zeros((slot_count, token_count), jnp.float32)
    weight = jnp.zeros((slot_count, token_count), jnp.float32)
    for at in range(top_count):
        named = ids_ref[at : at + 1, :] == expert_of
        chosen = jnp.where(named, 1.0, chosen)
        weight = jnp.where(named, weight_ref[at : at + 1, :], weight)
    before = lax.broadcasted_iota(jnp.int32, (token_count, token_count), 0)
    token = lax.broadcasted_iota(jnp.int32, (token_count, token_count), 1)
    earlier = jnp.where(before < token, 1.0, 0.0).astype(jnp.bfloat16)
    rank = jnp.dot(chosen.astype(jnp.bfloat16), earlier, preferred_element_type=jnp.float32)
    placed = jnp.where(rank == (row & 7).astype(jnp.float32), chosen, 0.0)
    mixing_ref[...] = placed * weight
    outgoing = jnp.dot(
        placed.astype(jnp.bfloat16), tokens_ref[...], preferred_element_type=jnp.float32
    )
    for at in range(EXPERTS):
        sends[at][:, :model_width] = outgoing[at * CAP : (at + 1) * CAP].astype(jnp.bfloat16)
    page_count, width = old_ref.shape
    row_count = EXPERTS * PER_PAIR * SPLIT
    out_row = lax.broadcasted_iota(jnp.int32, (row_count, page_count), 0)
    old_page = lax.broadcasted_iota(jnp.int32, (row_count, page_count), 1)
    tag_row = lax.broadcasted_iota(jnp.int32, (row_count, LANES), 0)
    select = [jnp.zeros((row_count, page_count), jnp.float32) for _ in range(SPLIT)]
    tags = jnp.zeros((row_count, LANES), jnp.float32)
    targets = [target_ref[at] for at in range(page_count)]
    peers = [jnp.where(target >= 0, target // page_span, -1) for target in targets]
    for at in range(page_count):
        rank_at = jnp.int32(0)
        for first in range(at):
            rank_at = rank_at + jnp.where(peers[first] == peers[at], 1, 0)
        row_at = ((peers[at] ^ me) * PER_PAIR + rank_at) * SPLIT
        row_at = jnp.where(peers[at] >= 0, row_at, -SPLIT)
        for part in range(SPLIT):
            here = (out_row == row_at + part) & (old_page == at)
            select[part] = jnp.where(here, 1.0, select[part])
        slot_tag = (targets[at] % page_count + 1).astype(jnp.float32)
        tags = jnp.where((tag_row >= row_at) & (tag_row < row_at + SPLIT), slot_tag, tags)
    width = width // SPLIT
    moved = jnp.zeros((row_count, width), jnp.float32)
    for part in range(SPLIT):
        columns = slice(part * width, (part + 1) * width)
        moved = moved + jnp.dot(
            select[part].astype(jnp.bfloat16),
            old_ref[:, columns],
            preferred_element_type=jnp.float32,
        )
    for at in range(EXPERTS):
        rows = slice(at * PER_PAIR * SPLIT, (at + 1) * PER_PAIR * SPLIT)
        page = jnp.concatenate([moved[rows], tags[rows]], axis=1).astype(jnp.bfloat16)
        if at == 1:
            sends[at][:, model_width:] = page
        else:
            pages[at - (at > 1)][...] = page


def open_work(ids, weights, tokens, old_latents, old_target, shard):
    token_count, model_width = tokens.shape
    page_count, page_width = old_latents.shape
    send = jax.ShapeDtypeStruct((CAP, model_width), jnp.bfloat16)
    mixing = jax.ShapeDtypeStruct((EXPERTS * CAP, token_count), jnp.float32)
    page = jax.ShapeDtypeStruct((PER_PAIR * SPLIT, page_width // SPLIT + LANES), jnp.bfloat16)
    longer = jax.ShapeDtypeStruct((CAP, model_width + page.shape[1]), jnp.bfloat16)
    across = jax.ShapeDtypeStruct((token_count, 2 * shard), jnp.bfloat16)
    spec = pl.BlockSpec(memory_space=VMEM)
    inputs = [
        pltpu.with_memory_space_constraint(value, pltpu.HBM)
        for value in (ids, weights, tokens, old_latents, old_target)
    ]
    results = pl.pallas_call(
        functools.partial(open_kernel, page_count * lax.axis_size("dp")),
        out_shape=(send, longer, send, send, mixing) + (page,) * (EXPERTS - 1) + (across,),
        in_specs=[pl.BlockSpec(memory_space=pltpu.HBM)] * 5,
        out_specs=(spec,) * (2 * EXPERTS + 1),
        scratch_shapes=[VMEM(value.shape, value.dtype) for value in inputs[:4]]
        + [
            SMEM(old_target.shape, old_target.dtype),
            pltpu.SemaphoreType.DMA((5,)),
        ],
        compiler_params=pltpu.CompilerParams(vmem_limit_bytes=8 << 20),
        cost_estimate=pl.CostEstimate(
            flops=20_000_000_000, bytes_accessed=2 << 20, transcendentals=0
        ),
        name="open",
    )(*inputs)
    sends, mixing, rest = results[:EXPERTS], results[EXPERTS], results[EXPERTS + 1 :]
    return sends, mixing, rest[: EXPERTS - 1], rest[EXPERTS - 1]


def stacked_rows(refs):
    return jnp.concatenate([ref[...].astype(jnp.float32) for ref in refs], axis=0).astype(
        jnp.bfloat16
    )


def gate_kernel(*refs):
    rows, gate_ref, out_ref = refs[:EXPERTS], refs[EXPERTS], refs[-1]
    block = stacked_rows([row.at[:, : gate_ref.shape[0]] for row in rows])
    for at in range(0, gate_ref.shape[1], CHUNK):
        columns = slice(at, at + CHUNK)
        out_ref[:, columns] = jnp.dot(
            block, gate_ref[:, columns], preferred_element_type=jnp.float32
        )


def gates(rows, w_gate, after):
    spec, unread = pl.BlockSpec(memory_space=VMEM), pl.BlockSpec(memory_space=pl.ANY)
    model_width, unit_count = w_gate.shape
    row_count = EXPERTS * CAP
    return pl.pallas_call(
        gate_kernel,
        out_shape=jax.ShapeDtypeStruct((row_count, unit_count), jnp.float32),
        in_specs=[spec] * (EXPERTS + 1) + [unread] * len(after),
        out_specs=spec,
        compiler_params=pltpu.CompilerParams(vmem_limit_bytes=4 << 20),
        cost_estimate=pl.CostEstimate(
            flops=4 * row_count * model_width * unit_count,
            bytes_accessed=4 * model_width * unit_count,
            transcendentals=0,
        ),
        name="gates",
    )(*rows, pltpu.with_memory_space_constraint(w_gate, VMEM), *after)


def expert_kernel(*refs):
    rows, refs = refs[:EXPERTS], refs[EXPERTS:]
    gates_ref, up_ref, down_ref = refs[:3]
    pages, outs, hidden_ref = refs[3:5], refs[-EXPERTS - 1 : -1], refs[-1]
    model_width = down_ref.shape[1]
    for out, page in zip(outs[2:], pages):
        out[:, model_width:] = page[...]
    block = stacked_rows([row.at[:, :model_width] for row in rows])
    for at in range(0, up_ref.shape[1], CHUNK):
        columns = slice(at, at + CHUNK)
        gate = gates_ref[:, columns]
        up = jnp.dot(block, up_ref[:, columns], preferred_element_type=jnp.float32)
        hidden_ref[:, columns] = (gate / (1.0 + jnp.exp(-gate)) * up).astype(jnp.bfloat16)
    for at in range(0, model_width, CHUNK):
        columns = slice(at, at + CHUNK)
        result = jnp.dot(
            hidden_ref[...], down_ref[:, columns], preferred_element_type=jnp.float32
        )
        for peer in range(EXPERTS):
            part = result[peer * CAP : (peer + 1) * CAP]
            outs[peer][:, columns] = part.astype(jnp.bfloat16)


def experts(rows, gate, w_up, w_down, pages, after):
    spec, unread = pl.BlockSpec(memory_space=VMEM), pl.BlockSpec(memory_space=pl.ANY)
    held = [pltpu.with_memory_space_constraint(w, VMEM) for w in (w_up, w_down)]
    unit_count, model_width = w_down.shape
    row_count = EXPERTS * CAP
    return pl.pallas_call(
        expert_kernel,
        out_shape=tuple(
            jax.ShapeDtypeStruct((CAP, model_width + extra), jnp.bfloat16)
            for extra in (0, 0, pages[0].shape[1], pages[1].shape[1])
        ),
        in_specs=[spec] * (5 + EXPERTS) + [unread] * len(after),
        out_specs=(spec,) * EXPERTS,
        scratch_shapes=[VMEM((row_count, unit_count), jnp.bfloat16)],
        compiler_params=pltpu.CompilerParams(vmem_limit_bytes=4 << 20),
        cost_estimate=pl.CostEstimate(
            flops=2 * row_count * model_width * unit_count,
            bytes_accessed=2 * model_width * unit_count,
            transcendentals=0,
        ),
        name="experts",
    )(*rows, gate, *held, *pages, *after)


def combine_kernel(mixing_ref, *refs):
    rows, parts = refs[:EXPERTS], refs[EXPERTS : EXPERTS + 2]
    rows = [rows[ORDER.index(at)] for at in range(EXPERTS)]
    out_ref, carried_ref, held_ref, sems = refs[EXPERTS + 2 :]
    model_width = out_ref.shape[1]
    mixing = mixing_ref[...]
    high = mixing.astype(jnp.bfloat16).astype(jnp.float32)
    mixing = jnp.concatenate([high, mixing - high], axis=0).astype(jnp.bfloat16)
    block = jnp.concatenate([stacked_rows([row.at[:, :model_width] for row in rows])] * 2, axis=0)
    width = model_width // PIECES
    copies = []
    for at in range(PIECES):
        columns = slice(at * width, (at + 1) * width)
        total = lax.dot_general(mixing, block[:, columns], TN, preferred_element_type=jnp.float32)
        held_ref[:, columns] = total.astype(jnp.bfloat16)
        copies.append(
            pltpu.make_async_copy(held_ref.at[:, columns], out_ref.at[:, columns], sems.at[at])
        )
        copies[-1].start()
    page_count, page_width = carried_ref.shape
    part_width = page_width // SPLIT
    arrivals = stacked_rows(
        [parts[0]] + [row.at[:, model_width:] for row in (parts[1], rows[2], rows[3])]
    )
    row_count = arrivals.shape[0]
    slot = lax.broadcasted_iota(jnp.int32, (row_count, page_count), 1).astype(jnp.float32)
    part_of = lax.broadcasted_iota(jnp.int32, (row_count, page_count), 0) % SPLIT
    meant = arrivals[:, part_width:].astype(jnp.float32)[:, :1] == slot + 1.0
    for part in range(SPLIT):
        chosen = lax.dot_general(
            jnp.where(meant & (part_of == part), 1.0, 0.0).astype(jnp.bfloat16),
            arrivals[:, :part_width],
            TN,
            preferred_element_type=jnp.float32,
        )
        columns = slice(part * part_width, (part + 1) * part_width)
        carried_ref[:, columns] = chosen.astype(jnp.bfloat16)
    for copy in copies:
        copy.wait()


def combine(mixing, rows, own_pages, near_rows, page_count):
    slot_count, token_count = mixing.shape
    model_width = rows[0].shape[1]
    page_width = (own_pages.shape[1] - LANES) * SPLIT
    spec = pl.BlockSpec(memory_space=VMEM)
    return pl.pallas_call(
        combine_kernel,
        out_shape=(
            jax.ShapeDtypeStruct((token_count, model_width), jnp.bfloat16),
            jax.ShapeDtypeStruct((page_count, page_width), jnp.bfloat16),
        ),
        in_specs=[spec] * (3 + EXPERTS),
        out_specs=(pl.BlockSpec(memory_space=pltpu.HBM), spec),
        scratch_shapes=[
            VMEM((token_count, model_width), jnp.bfloat16),
            pltpu.SemaphoreType.DMA((PIECES,)),
        ],
        compiler_params=pltpu.CompilerParams(vmem_limit_bytes=8 << 20),
        cost_estimate=pl.CostEstimate(
            flops=11530000000,
            bytes_accessed=3 * token_count * model_width,
            transcendentals=0,
        ),
        name="combine",
    )(mixing, *(rows[at] for at in ORDER), own_pages, near_rows)


def project_kernel(tokens_ref, theirs_ref, own_ref, *refs):
    held, (mine_out, theirs_out) = refs[:4], refs[-4:-2]
    both_ref, far_ref = refs[-2:]
    group, me, dp = (lax.axis_index(axis) for axis in ("groups", "expert", "dp"))
    shard = own_ref.shape[1]
    chip_rows, _ = piece_rows(own_ref.shape[0])
    chip, core = group * 2 + dp // 2, dp % 2

    def assemble(my_core):
        orders = ((0, 1, 2, 3), (0, 2, 1, 3))
        for chip_xor in range(4):
            halves = []
            for core_at in range(2):
                at = orders[core_at].index(chip_xor)
                buffer = held[at // 2 + (0 if core_at == my_core else 2)]
                halves.append(buffer[at % 2].astype(jnp.float32))
            rows = pl.ds(pl.multiple_of((chip ^ chip_xor) * chip_rows, ROWS), chip_rows)
            far_ref[rows, :] = jnp.concatenate(halves, axis=0).astype(jnp.bfloat16)

    for my_core in range(2):
        pl.when(core == my_core)(functools.partial(assemble, my_core))

    def part(weights_ref, tokens):
        return lax.dot_general(weights_ref[...], tokens, NT, preferred_element_type=jnp.float32)

    count = tokens_ref.shape[0]
    for half, bit in enumerate((0, 2)):
        columns = pl.ds(pl.multiple_of((me ^ bit) * shard, LANES), shard)
        both_ref[:count, half * shard : (half + 1) * shard] = tokens_ref[:, columns]
    both_ref[count:, :] = theirs_ref[...]
    total = part(own_ref, both_ref[:, :shard])
    total = total + part(far_ref, both_ref[:, shard:])
    mine_out[...] = total[:, :count]
    theirs_out[...] = total[:, count:].astype(jnp.bfloat16)


def project(tokens, theirs, own, held):
    spec = pl.BlockSpec(memory_space=VMEM)
    token_count = tokens.shape[0]
    width, shard = own.shape
    return pl.pallas_call(
        project_kernel,
        out_shape=(
            jax.ShapeDtypeStruct((width, token_count), jnp.float32),
            jax.ShapeDtypeStruct((width, token_count), jnp.bfloat16),
        ),
        in_specs=[spec] * 7,
        out_specs=(spec, spec),
        scratch_shapes=[
            VMEM((2 * token_count, 2 * shard), jnp.bfloat16),
            VMEM((width, shard), jnp.bfloat16),
        ],
        compiler_params=pltpu.CompilerParams(vmem_limit_bytes=8 << 20),
        cost_estimate=pl.CostEstimate(flops=1153000000, bytes_accessed=0, transcendentals=0),
        name="project",
    )(tokens, theirs, own, *held)


def finish_kernel(mine_ref, theirs_ref, gain_ref, unread_ref, out_ref):
    del unread_ref
    page_count = out_ref.shape[0]
    projected = mine_ref[...] + theirs_ref[...].astype(jnp.float32)
    nope_part = projected[:KV]
    inv_rms = lax.rsqrt(jnp.mean(nope_part * nope_part, axis=0, keepdims=True) + EPS)
    scaled = jnp.concatenate([nope_part * inv_rms, projected[KV:]], axis=0)
    high = scaled.astype(jnp.bfloat16)
    low = (scaled - high.astype(jnp.float32)).astype(jnp.bfloat16)
    width, token_count = scaled.shape
    page_tokens = token_count // page_count
    row = lax.broadcasted_iota(jnp.int32, (token_count, token_count), 0)
    source = lax.broadcasted_iota(jnp.int32, (token_count, token_count), 1)
    moves = source == (row % page_count) * page_tokens + row // page_count
    moves = jnp.where(moves, 1.0, 0.0).astype(jnp.bfloat16)
    ordered = lax.dot_general(
        jnp.concatenate([moves, moves], axis=1),
        jnp.concatenate([high, low], axis=1),
        NT,
        preferred_element_type=jnp.float32,
    )
    ordered = jnp.concatenate([ordered[:, :KV] * gain_ref[...], ordered[:, KV:]], axis=1)
    for at in range(0, page_tokens, 2):
        fresh = jnp.concatenate(
            [ordered[(at + half) * page_count : (at + half + 1) * page_count] for half in range(2)],
            axis=1,
        )
        out_ref[:, at * width : (at + 2) * width] = fresh.astype(jnp.bfloat16)


def finish(mine, theirs, latent_gain, carried):
    vmem = pl.BlockSpec(memory_space=VMEM)
    return pl.pallas_call(
        finish_kernel,
        out_shape=jax.ShapeDtypeStruct(carried.shape, jnp.bfloat16),
        in_specs=[vmem] * 3 + [pl.BlockSpec(memory_space=pl.ANY)],
        out_specs=vmem,
        compiler_params=pltpu.CompilerParams(vmem_limit_bytes=6 << 20),
        cost_estimate=pl.CostEstimate(
            flops=4 * mine.shape[1] ** 2 * mine.shape[0],
            bytes_accessed=1 << 20,
            transcendentals=mine.shape[1],
        ),
        name="finish",
    )(mine, theirs, latent_gain.reshape(1, -1), carried)


def swap(value, axis, bit):
    return lax.ppermute(value, axis, xor_pairs(lax.axis_size(axis), bit))


def tied(value, *after):
    return lax.optimization_barrier((value, *after))[0]


def exchanged(values, axis="expert"):
    return [values[0]] + [swap(values[bit], axis, bit) for bit in range(1, len(values))]


def block_shards(
    tokens,
    w_gate,
    w_up,
    w_down,
    w_latent,
    latent_gain,
    route_ids,
    route_weight,
    old_latents,
    survive,
    old_target,
):
    group_count, dp_count = lax.axis_size("groups"), lax.axis_size("dp")
    plane = ("groups", "dp")
    latent = w_latent.T
    at = lax.axis_index("groups") * 2 + lax.axis_index("dp") // 2
    chip_rows, core_rows = piece_rows(latent.shape[0])
    start = at * chip_rows + lax.axis_index("dp") % 2 * core_rows
    piece = lax.dynamic_slice_in_dim(latent, start, core_rows, axis=0)
    far_piece = swap(piece, "expert", 2)
    sends, mixing, (own_pages, *pages), across = open_work(
        route_ids.T, route_weight.T, tokens, old_latents, old_target, latent.shape[1]
    )
    received = exchanged(sends)
    first = lax.ppermute(far_piece, plane, plane_pairs(group_count, dp_count, True))
    theirs = swap(tied(across, far_piece), "expert", 1)
    gate = gates(received, w_gate, (far_piece,))
    near = tied(jnp.stack([far_piece, first]), gate)
    far = lax.ppermute(near, plane, plane_pairs(group_count, dp_count, False))
    near_other = swap(near, "dp", 1)
    results = experts(received, gate, w_up, w_down, pages, (near,))
    results = [tied(result, theirs, far) for result in results]
    returned = exchanged(results)
    far = tied(far, results[0])
    far_other = swap(far, "dp", 1)
    mine, across_sums = project(
        tokens, theirs, latent, (near, far, near_other, far_other)
    )
    their_sums = swap(across_sums, "expert", 1)
    moe_out, carried = combine(mixing, returned, own_pages, received[1], old_latents.shape[0])
    fresh = finish(mine, their_sums, latent_gain, carried)
    latents = jnp.where((survive > 0)[:, None], carried, fresh)
    return (moe_out, latents)


def rebuild_latents(tokens, w_latent, latent_gain):
    projected = jnp.dot(
        tokens,
        lax.all_gather(w_latent, "expert", axis=0, tiled=True),
        preferred_element_type=jnp.float32,
    )
    nope_part = projected[:, :KV]
    inv_rms = lax.rsqrt(jnp.mean(nope_part * nope_part, axis=1, keepdims=True) + EPS)
    return jnp.concatenate([nope_part * inv_rms * latent_gain, projected[:, KV:]], axis=1).astype(
        jnp.bfloat16
    )


def moved_pages(old_latents, survive, old_target, rebuilt):
    peer_count = lax.axis_size("expert")
    dp_count = lax.axis_size("dp")
    page_count = old_latents.shape[0]
    per_pair = max(1, page_count // peer_count)
    slot_ids = jnp.arange(page_count, dtype=jnp.int32)
    peer_ids = jnp.arange(peer_count, dtype=jnp.int32)
    rank_ids = jnp.arange(per_pair, dtype=jnp.int32)
    valid_out = old_target >= 0
    target_peer = old_target // page_count // dp_count
    target_slot = jnp.where(valid_out, old_target % page_count + 1, 0).astype(jnp.float32)
    same_peer = (target_peer[:, None] == target_peer[None, :]) & valid_out[None, :]
    earlier = slot_ids[None, :] < slot_ids[:, None]
    out_rank = jnp.sum((same_peer & earlier).astype(jnp.int32), axis=1)
    select = (
        valid_out[None, None, :]
        & (target_peer[None, None, :] == peer_ids[:, None, None])
        & (out_rank[None, None, :] == rank_ids[None, :, None])
    )
    select = select.reshape(peer_count * per_pair, page_count)
    outgoing = jnp.dot(
        select.astype(jnp.bfloat16), old_latents, preferred_element_type=jnp.float32
    ).astype(jnp.bfloat16)
    slot_tags = jnp.dot(
        select.astype(jnp.float32), target_slot, precision=lax.Precision.HIGHEST
    ).astype(jnp.bfloat16)
    arrived, arrived_tags = (
        lax.all_to_all(
            outgoing.reshape(peer_count, per_pair, -1),
            "expert",
            split_axis=0,
            concat_axis=0,
            tiled=True,
        ),
        lax.all_to_all(
            slot_tags.reshape(peer_count, per_pair),
            "expert",
            split_axis=0,
            concat_axis=0,
            tiled=True,
        ),
    )
    tag_values = arrived_tags.reshape(peer_count * per_pair).astype(jnp.float32)
    chooser = (tag_values[None, :] == (slot_ids + 1).astype(jnp.float32)[:, None]).astype(
        jnp.bfloat16
    )
    carried = jnp.dot(
        chooser, arrived.reshape(peer_count * per_pair, -1), preferred_element_type=jnp.float32
    ).astype(jnp.bfloat16)
    return jnp.where((survive > 0)[:, None], carried, rebuilt)


def route_tables(route_ids, route_weight):
    token_count, top_count = route_ids.shape
    flat_ids = route_ids.reshape(-1)
    onehot = (flat_ids[:, None] == jnp.arange(EXPERTS, dtype=jnp.int32)[None, :]).astype(jnp.int32)
    slot_rank = jnp.sum((jnp.cumsum(onehot, axis=0) - onehot) * onehot, axis=1)
    slot_index = jnp.where(flat_ids < EXPERTS, flat_ids * CAP + slot_rank, -1)
    matches = slot_index[:, None] == jnp.arange(EXPERTS * CAP, dtype=jnp.int32)[None, :]
    matches = matches.reshape(token_count, top_count, EXPERTS * CAP)
    placing = jnp.sum(matches.astype(jnp.float32), axis=1).astype(jnp.bfloat16)
    mixing = jnp.sum(matches.astype(jnp.float32) * route_weight[:, :, None], axis=1)
    return (placing, mixing)


def expert_rows(received, w_gate, w_up, w_down, per_dev):
    unit_count = w_gate.shape[1] // per_dev
    gate_w = w_gate.reshape(w_gate.shape[0], per_dev, unit_count)
    up_w = w_up.reshape(w_up.shape[0], per_dev, unit_count)
    down_w = w_down.reshape(per_dev, unit_count, w_down.shape[1])
    gate_value = jnp.einsum("spkd,dpf->spkf", received, gate_w, preferred_element_type=jnp.float32)
    up_value = jnp.einsum("spkd,dpf->spkf", received, up_w, preferred_element_type=jnp.float32)
    hidden = (jax.nn.silu(gate_value) * up_value).astype(jnp.bfloat16)
    return jnp.einsum("spkf,pfd->spkd", hidden, down_w, preferred_element_type=jnp.float32)


def shards(
    tokens,
    w_gate,
    w_up,
    w_down,
    w_latent,
    latent_gain,
    route_ids,
    route_weight,
    old_latents,
    survive,
    old_target,
):
    rebuilt = rebuild_latents(tokens, w_latent, latent_gain).reshape(old_latents.shape[0], -1)
    latents = moved_pages(old_latents, survive, old_target, rebuilt)
    column_count = w_gate.shape[1]
    per_dev = max(1, column_count // FF)
    span_size = max(1, FF // column_count)
    group_count = EXPERTS // per_dev
    model_width = tokens.shape[1]
    placing, mixing = route_tables(route_ids, route_weight)
    outgoing = jnp.einsum("te,td->ed", placing, tokens, preferred_element_type=jnp.float32).astype(
        jnp.bfloat16
    )
    grouped = outgoing.reshape(group_count, per_dev, CAP, model_width)
    sent_rows = jnp.repeat(grouped, span_size, axis=0)
    partial_value = expert_rows(
        lax.all_to_all(sent_rows, "expert", split_axis=0, concat_axis=0, tiled=True),
        w_gate,
        w_up,
        w_down,
        per_dev,
    )
    returned = lax.all_to_all(
        partial_value.astype(jnp.bfloat16), "expert", split_axis=0, concat_axis=0, tiled=True
    ).astype(partial_value.dtype)
    summed = jnp.sum(returned.reshape(group_count, span_size, per_dev, CAP, model_width), axis=1)
    expert_out = summed.reshape(EXPERTS * CAP, model_width)
    moe_out = jnp.dot(mixing, expert_out, precision=lax.Precision.HIGHEST).astype(jnp.bfloat16)
    return (moe_out, latents)


def small_block(mesh):
    sizes = (mesh.shape["groups"], mesh.shape["expert"], mesh.shape["dp"])
    return sizes == (2, EXPERTS, 4)


def solution(mesh):
    in_specs = (
        P(("groups", "expert", "dp"), None),
        P(None, "expert"),
        P(None, "expert"),
        P("expert", None),
        P("expert", None),
        P(),
        P(("groups", "expert", "dp"), None),
        P(("groups", "expert", "dp"), None),
        P(("groups", "expert", "dp"), None),
        P(("groups", "expert", "dp")),
        P(("groups", "expert", "dp")),
    )
    out_specs = (P(("groups", "expert", "dp"), None), P(("groups", "expert", "dp"), None))
    body = block_shards if small_block(mesh) else shards
    return jax.shard_map(body, mesh=mesh, in_specs=in_specs, out_specs=out_specs, check_vma=False)
```

```python
import functools

import jax
import jax.numpy as jnp
from jax import lax
from jax.experimental import pallas as pl
from jax.experimental.pallas import tpu as pltpu
from jax.sharding import PartitionSpec as P

FF = 2048
EXPERTS = 4
KV = 512
CAP = 8
PER_PAIR = 2
SPLIT = 4
LANES = 128
ROWS = 16


EPS = 1e-06
VMEM = pltpu.VMEM
SMEM = pltpu.SMEM
CHUNK = 512
PIECES = 7
ORDER = (0, 3, 1, 2)
NT = (((1,), (1,)), ((), ()))
TN = (((0,), (0,)), ((), ()))


def xor_pairs(count, bit):
    return [(at, at ^ bit) for at in range(count)]


def plane_pairs(group_count, dp_count, core_zero_along_x):
    pairs = []
    for group in range(group_count):
        for dp in range(dp_count):
            along_x = (dp % 2 == 0) == core_zero_along_x
            to_group, to_dp = (group, dp ^ 2) if along_x else (group ^ 1, dp)
            pairs.append((group * dp_count + dp, to_group * dp_count + to_dp))
    return pairs


def piece_rows(width):
    return width // 4, width // 8


def open_kernel(page_span, *refs):
    sources, outs = refs[:5], refs[5:]
    sends, mixing_ref, pages = outs[:EXPERTS], outs[EXPERTS], outs[EXPERTS + 1 : 2 * EXPERTS]
    across_ref = outs[2 * EXPERTS]
    *held, sems = outs[2 * EXPERTS + 1 :]
    model_width = sends[0].shape[1]
    ids_ref, weight_ref, tokens_ref, old_ref, target_ref = held
    copies = [
        pltpu.make_async_copy(source, target, sems.at[at])
        for at, (source, target) in enumerate(zip(sources, held))
    ]
    for copy in copies:
        copy.start()
    me = lax.axis_index("expert")
    for copy in copies:
        copy.wait()
    shard = across_ref.shape[1] // 2
    for half, bit in enumerate((1, 3)):
        columns = pl.ds(pl.multiple_of((me ^ bit) * shard, LANES), shard)
        across_ref[:, half * shard : (half + 1) * shard] = tokens_ref[:, columns]
    top_count, token_count = ids_ref.shape
    slot_count = EXPERTS * CAP
    row = lax.broadcasted_iota(jnp.int32, (slot_count, token_count), 0)
    expert_of = (row >> 3) ^ me
    chosen = jnp.zeros((slot_count, token_count), jnp.float32)
    weight = jnp.zeros((slot_count, token_count), jnp.float32)
    for at in range(top_count):
        named = ids_ref[at : at + 1, :] == expert_of
        chosen = jnp.where(named, 1.0, chosen)
        weight = jnp.where(named, weight_ref[at : at + 1, :], weight)
    before = lax.broadcasted_iota(jnp.int32, (token_count, token_count), 0)
    token = lax.broadcasted_iota(jnp.int32, (token_count, token_count), 1)
    earlier = jnp.where(before < token, 1.0, 0.0).astype(jnp.bfloat16)
    rank = jnp.dot(chosen.astype(jnp.bfloat16), earlier, preferred_element_type=jnp.float32)
    placed = jnp.where(rank == (row & 7).astype(jnp.float32), chosen, 0.0)
    mixing_ref[...] = placed * weight
    outgoing = jnp.dot(
        placed.astype(jnp.bfloat16), tokens_ref[...], preferred_element_type=jnp.float32
    )
    for at in range(EXPERTS):
        sends[at][:, :model_width] = outgoing[at * CAP : (at + 1) * CAP].astype(jnp.bfloat16)
    page_count, width = old_ref.shape
    row_count = EXPERTS * PER_PAIR * SPLIT
    out_row = lax.broadcasted_iota(jnp.int32, (row_count, page_count), 0)
    old_page = lax.broadcasted_iota(jnp.int32, (row_count, page_count), 1)
    tag_row = lax.broadcasted_iota(jnp.int32, (row_count, LANES), 0)
    select = [jnp.zeros((row_count, page_count), jnp.float32) for _ in range(SPLIT)]
    tags = jnp.zeros((row_count, LANES), jnp.float32)
    targets = [target_ref[at] for at in range(page_count)]
    peers = [jnp.where(target >= 0, target // page_span, -1) for target in targets]
    for at in range(page_count):
        rank_at = jnp.int32(0)
        for first in range(at):
            rank_at = rank_at + jnp.where(peers[first] == peers[at], 1, 0)
        row_at = ((peers[at] ^ me) * PER_PAIR + rank_at) * SPLIT
        row_at = jnp.where(peers[at] >= 0, row_at, -SPLIT)
        for part in range(SPLIT):
            here = (out_row == row_at + part) & (old_page == at)
            select[part] = jnp.where(here, 1.0, select[part])
        slot_tag = (targets[at] % page_count + 1).astype(jnp.float32)
        tags = jnp.where((tag_row >= row_at) & (tag_row < row_at + SPLIT), slot_tag, tags)
    width = width // SPLIT
    moved = jnp.zeros((row_count, width), jnp.float32)
    for part in range(SPLIT):
        columns = slice(part * width, (part + 1) * width)
        moved = moved + jnp.dot(
            select[part].astype(jnp.bfloat16),
            old_ref[:, columns],
            preferred_element_type=jnp.float32,
        )
    for at in range(EXPERTS):
        rows = slice(at * PER_PAIR * SPLIT, (at + 1) * PER_PAIR * SPLIT)
        page = jnp.concatenate([moved[rows], tags[rows]], axis=1).astype(jnp.bfloat16)
        if at == 1:
            sends[at][:, model_width:] = page
        else:
            pages[at - (at > 1)][...] = page


def open_work(ids, weights, tokens, old_latents, old_target, shard):
    token_count, model_width = tokens.shape
    page_count, page_width = old_latents.shape
    send = jax.ShapeDtypeStruct((CAP, model_width), jnp.bfloat16)
    mixing = jax.ShapeDtypeStruct((EXPERTS * CAP, token_count), jnp.float32)
    page = jax.ShapeDtypeStruct((PER_PAIR * SPLIT, page_width // SPLIT + LANES), jnp.bfloat16)
    longer = jax.ShapeDtypeStruct((CAP, model_width + page.shape[1]), jnp.bfloat16)
    across = jax.ShapeDtypeStruct((token_count, 2 * shard), jnp.bfloat16)
    spec = pl.BlockSpec(memory_space=VMEM)
    inputs = [
        pltpu.with_memory_space_constraint(value, pltpu.HBM)
        for value in (ids, weights, tokens, old_latents, old_target)
    ]
    results = pl.pallas_call(
        functools.partial(open_kernel, page_count * lax.axis_size("dp")),
        out_shape=(send, longer, send, send, mixing) + (page,) * (EXPERTS - 1) + (across,),
        in_specs=[pl.BlockSpec(memory_space=pltpu.HBM)] * 5,
        out_specs=(spec,) * (2 * EXPERTS + 1),
        scratch_shapes=[VMEM(value.shape, value.dtype) for value in inputs[:4]]
        + [
            SMEM(old_target.shape, old_target.dtype),
            pltpu.SemaphoreType.DMA((5,)),
        ],
        compiler_params=pltpu.CompilerParams(vmem_limit_bytes=8 << 20),
        cost_estimate=pl.CostEstimate(
            flops=20_000_000_000, bytes_accessed=2 << 20, transcendentals=0
        ),
        name="open",
    )(*inputs)
    sends, mixing, rest = results[:EXPERTS], results[EXPERTS], results[EXPERTS + 1 :]
    return sends, mixing, rest[: EXPERTS - 1], rest[EXPERTS - 1]


def stacked_rows(refs):
    return jnp.concatenate([ref[...].astype(jnp.float32) for ref in refs], axis=0).astype(
        jnp.bfloat16
    )


def gate_kernel(*refs):
    rows, gate_ref, out_ref = refs[:EXPERTS], refs[EXPERTS], refs[-1]
    block = stacked_rows([row.at[:, : gate_ref.shape[0]] for row in rows])
    for at in range(0, gate_ref.shape[1], CHUNK):
        columns = slice(at, at + CHUNK)
        out_ref[:, columns] = jnp.dot(
            block, gate_ref[:, columns], preferred_element_type=jnp.float32
        )


def gates(rows, w_gate, after):
    spec, unread = pl.BlockSpec(memory_space=VMEM), pl.BlockSpec(memory_space=pl.ANY)
    model_width, unit_count = w_gate.shape
    row_count = EXPERTS * CAP
    return pl.pallas_call(
        gate_kernel,
        out_shape=jax.ShapeDtypeStruct((row_count, unit_count), jnp.float32),
        in_specs=[spec] * (EXPERTS + 1) + [unread] * len(after),
        out_specs=spec,
        compiler_params=pltpu.CompilerParams(vmem_limit_bytes=4 << 20),
        cost_estimate=pl.CostEstimate(
            flops=4 * row_count * model_width * unit_count,
            bytes_accessed=4 * model_width * unit_count,
            transcendentals=0,
        ),
        name="gates",
    )(*rows, pltpu.with_memory_space_constraint(w_gate, VMEM), *after)


def expert_kernel(*refs):
    rows, refs = refs[:EXPERTS], refs[EXPERTS:]
    gates_ref, up_ref, down_ref = refs[:3]
    pages, outs, hidden_ref = refs[3:5], refs[-EXPERTS - 1 : -1], refs[-1]
    model_width = down_ref.shape[1]
    for out, page in zip(outs[2:], pages):
        out[:, model_width:] = page[...]
    block = stacked_rows([row.at[:, :model_width] for row in rows])
    for at in range(0, up_ref.shape[1], CHUNK):
        columns = slice(at, at + CHUNK)
        gate = gates_ref[:, columns]
        up = jnp.dot(block, up_ref[:, columns], preferred_element_type=jnp.float32)
        hidden_ref[:, columns] = (gate / (1.0 + jnp.exp(-gate)) * up).astype(jnp.bfloat16)
    for at in range(0, model_width, CHUNK):
        columns = slice(at, at + CHUNK)
        result = jnp.dot(
            hidden_ref[...], down_ref[:, columns], preferred_element_type=jnp.float32
        )
        for peer in range(EXPERTS):
            part = result[peer * CAP : (peer + 1) * CAP]
            outs[peer][:, columns] = part.astype(jnp.bfloat16)


def experts(rows, gate, w_up, w_down, pages, after):
    spec, unread = pl.BlockSpec(memory_space=VMEM), pl.BlockSpec(memory_space=pl.ANY)
    held = [pltpu.with_memory_space_constraint(w, VMEM) for w in (w_up, w_down)]
    unit_count, model_width = w_down.shape
    row_count = EXPERTS * CAP
    return pl.pallas_call(
        expert_kernel,
        out_shape=tuple(
            jax.ShapeDtypeStruct((CAP, model_width + extra), jnp.bfloat16)
            for extra in (0, 0, pages[0].shape[1], pages[1].shape[1])
        ),
        in_specs=[spec] * (5 + EXPERTS) + [unread] * len(after),
        out_specs=(spec,) * EXPERTS,
        scratch_shapes=[VMEM((row_count, unit_count), jnp.bfloat16)],
        compiler_params=pltpu.CompilerParams(vmem_limit_bytes=4 << 20),
        cost_estimate=pl.CostEstimate(
            flops=2 * row_count * model_width * unit_count,
            bytes_accessed=2 * model_width * unit_count,
            transcendentals=0,
        ),
        name="experts",
    )(*rows, gate, *held, *pages, *after)


def combine_kernel(mixing_ref, *refs):
    rows, parts = refs[:EXPERTS], refs[EXPERTS : EXPERTS + 2]
    rows = [rows[ORDER.index(at)] for at in range(EXPERTS)]
    out_ref, carried_ref, held_ref, sems = refs[EXPERTS + 2 :]
    model_width = out_ref.shape[1]
    mixing = mixing_ref[...]
    high = mixing.astype(jnp.bfloat16).astype(jnp.float32)
    mixing = jnp.concatenate([high, mixing - high], axis=0).astype(jnp.bfloat16)
    block = jnp.concatenate([stacked_rows([row.at[:, :model_width] for row in rows])] * 2, axis=0)
    width = model_width // PIECES
    copies = []
    for at in range(PIECES):
        columns = slice(at * width, (at + 1) * width)
        total = lax.dot_general(mixing, block[:, columns], TN, preferred_element_type=jnp.float32)
        held_ref[:, columns] = total.astype(jnp.bfloat16)
        copies.append(
            pltpu.make_async_copy(held_ref.at[:, columns], out_ref.at[:, columns], sems.at[at])
        )
        copies[-1].start()
    page_count, page_width = carried_ref.shape
    part_width = page_width // SPLIT
    arrivals = stacked_rows(
        [parts[0]] + [row.at[:, model_width:] for row in (parts[1], rows[2], rows[3])]
    )
    row_count = arrivals.shape[0]
    column = lax.broadcasted_iota(jnp.int32, (row_count, SPLIT * page_count), 1)
    slot = (column % page_count + 1).astype(jnp.float32)
    part_of = lax.broadcasted_iota(jnp.int32, (row_count, SPLIT * page_count), 0) % SPLIT
    meant = arrivals[:, part_width:].astype(jnp.float32)[:, :1] == slot
    chosen = lax.dot_general(
        jnp.where(meant & (part_of == column // page_count), 1.0, 0.0).astype(jnp.bfloat16),
        arrivals[:, :part_width],
        TN,
        preferred_element_type=jnp.float32,
    )
    for part in range(SPLIT):
        columns = slice(part * part_width, (part + 1) * part_width)
        rows = slice(part * page_count, (part + 1) * page_count)
        carried_ref[:, columns] = chosen[rows].astype(jnp.bfloat16)
    for copy in copies:
        copy.wait()


def combine(mixing, rows, own_pages, near_rows, page_count):
    slot_count, token_count = mixing.shape
    model_width = rows[0].shape[1]
    page_width = (own_pages.shape[1] - LANES) * SPLIT
    spec = pl.BlockSpec(memory_space=VMEM)
    return pl.pallas_call(
        combine_kernel,
        out_shape=(
            jax.ShapeDtypeStruct((token_count, model_width), jnp.bfloat16),
            jax.ShapeDtypeStruct((page_count, page_width), jnp.bfloat16),
        ),
        in_specs=[spec] * (3 + EXPERTS),
        out_specs=(pl.BlockSpec(memory_space=pltpu.HBM), spec),
        scratch_shapes=[
            VMEM((token_count, model_width), jnp.bfloat16),
            pltpu.SemaphoreType.DMA((PIECES,)),
        ],
        compiler_params=pltpu.CompilerParams(vmem_limit_bytes=8 << 20),
        cost_estimate=pl.CostEstimate(
            flops=11530000000,
            bytes_accessed=3 * token_count * model_width,
            transcendentals=0,
        ),
        name="combine",
    )(mixing, *(rows[at] for at in ORDER), own_pages, near_rows)


def project_kernel(tokens_ref, theirs_ref, own_ref, *refs):
    held, (mine_out, theirs_out) = refs[:4], refs[-4:-2]
    both_ref, far_ref = refs[-2:]
    group, me, dp = (lax.axis_index(axis) for axis in ("groups", "expert", "dp"))
    shard = own_ref.shape[1]
    chip_rows, _ = piece_rows(own_ref.shape[0])
    chip, core = group * 2 + dp // 2, dp % 2

    def assemble(my_core):
        orders = ((0, 1, 2, 3), (0, 2, 1, 3))
        for chip_xor in range(4):
            halves = []
            for core_at in range(2):
                at = orders[core_at].index(chip_xor)
                buffer = held[at // 2 + (0 if core_at == my_core else 2)]
                halves.append(buffer[at % 2].astype(jnp.float32))
            rows = pl.ds(pl.multiple_of((chip ^ chip_xor) * chip_rows, ROWS), chip_rows)
            far_ref[rows, :] = jnp.concatenate(halves, axis=0).astype(jnp.bfloat16)

    for my_core in range(2):
        pl.when(core == my_core)(functools.partial(assemble, my_core))

    def part(weights_ref, tokens):
        return lax.dot_general(weights_ref[...], tokens, NT, preferred_element_type=jnp.float32)

    count = tokens_ref.shape[0]
    for half, bit in enumerate((0, 2)):
        columns = pl.ds(pl.multiple_of((me ^ bit) * shard, LANES), shard)
        both_ref[:count, half * shard : (half + 1) * shard] = tokens_ref[:, columns]
    both_ref[count:, :] = theirs_ref[...]
    total = part(own_ref, both_ref[:, :shard])
    total = total + part(far_ref, both_ref[:, shard:])
    mine_out[...] = total[:, :count]
    theirs_out[...] = total[:, count:].astype(jnp.bfloat16)


def project(tokens, theirs, own, held):
    spec = pl.BlockSpec(memory_space=VMEM)
    token_count = tokens.shape[0]
    width, shard = own.shape
    return pl.pallas_call(
        project_kernel,
        out_shape=(
            jax.ShapeDtypeStruct((width, token_count), jnp.float32),
            jax.ShapeDtypeStruct((width, token_count), jnp.bfloat16),
        ),
        in_specs=[spec] * 7,
        out_specs=(spec, spec),
        scratch_shapes=[
            VMEM((2 * token_count, 2 * shard), jnp.bfloat16),
            VMEM((width, shard), jnp.bfloat16),
        ],
        compiler_params=pltpu.CompilerParams(vmem_limit_bytes=8 << 20),
        cost_estimate=pl.CostEstimate(flops=1153000000, bytes_accessed=0, transcendentals=0),
        name="project",
    )(tokens, theirs, own, *held)


def finish_kernel(mine_ref, theirs_ref, gain_ref, unread_ref, out_ref):
    del unread_ref
    page_count = out_ref.shape[0]
    projected = mine_ref[...] + theirs_ref[...].astype(jnp.float32)
    nope_part = projected[:KV]
    inv_rms = lax.rsqrt(jnp.mean(nope_part * nope_part, axis=0, keepdims=True) + EPS)
    scaled = jnp.concatenate([nope_part * inv_rms, projected[KV:]], axis=0)
    high = scaled.astype(jnp.bfloat16)
    low = (scaled - high.astype(jnp.float32)).astype(jnp.bfloat16)
    width, token_count = scaled.shape
    page_tokens = token_count // page_count
    row = lax.broadcasted_iota(jnp.int32, (token_count, token_count), 0)
    source = lax.broadcasted_iota(jnp.int32, (token_count, token_count), 1)
    moves = source == (row % page_count) * page_tokens + row // page_count
    moves = jnp.where(moves, 1.0, 0.0).astype(jnp.bfloat16)
    ordered = lax.dot_general(
        jnp.concatenate([moves, moves], axis=1),
        jnp.concatenate([high, low], axis=1),
        NT,
        preferred_element_type=jnp.float32,
    )
    ordered = jnp.concatenate([ordered[:, :KV] * gain_ref[...], ordered[:, KV:]], axis=1)
    for at in range(0, page_tokens, 2):
        fresh = jnp.concatenate(
            [ordered[(at + half) * page_count : (at + half + 1) * page_count] for half in range(2)],
            axis=1,
        )
        out_ref[:, at * width : (at + 2) * width] = fresh.astype(jnp.bfloat16)


def finish(mine, theirs, latent_gain, carried):
    vmem = pl.BlockSpec(memory_space=VMEM)
    return pl.pallas_call(
        finish_kernel,
        out_shape=jax.ShapeDtypeStruct(carried.shape, jnp.bfloat16),
        in_specs=[vmem] * 3 + [pl.BlockSpec(memory_space=pl.ANY)],
        out_specs=vmem,
        compiler_params=pltpu.CompilerParams(vmem_limit_bytes=6 << 20),
        cost_estimate=pl.CostEstimate(
            flops=4 * mine.shape[1] ** 2 * mine.shape[0],
            bytes_accessed=1 << 20,
            transcendentals=mine.shape[1],
        ),
        name="finish",
    )(mine, theirs, latent_gain.reshape(1, -1), carried)


def swap(value, axis, bit):
    return lax.ppermute(value, axis, xor_pairs(lax.axis_size(axis), bit))


def tied(value, *after):
    return lax.optimization_barrier((value, *after))[0]


def exchanged(values, axis="expert"):
    return [values[0]] + [swap(values[bit], axis, bit) for bit in range(1, len(values))]


def block_shards(
    tokens,
    w_gate,
    w_up,
    w_down,
    w_latent,
    latent_gain,
    route_ids,
    route_weight,
    old_latents,
    survive,
    old_target,
):
    group_count, dp_count = lax.axis_size("groups"), lax.axis_size("dp")
    plane = ("groups", "dp")
    latent = w_latent.T
    at = lax.axis_index("groups") * 2 + lax.axis_index("dp") // 2
    chip_rows, core_rows = piece_rows(latent.shape[0])
    start = at * chip_rows + lax.axis_index("dp") % 2 * core_rows
    piece = lax.dynamic_slice_in_dim(latent, start, core_rows, axis=0)
    far_piece = swap(piece, "expert", 2)
    sends, mixing, (own_pages, *pages), across = open_work(
        route_ids.T, route_weight.T, tokens, old_latents, old_target, latent.shape[1]
    )
    received = exchanged(sends)
    first = lax.ppermute(far_piece, plane, plane_pairs(group_count, dp_count, True))
    theirs = swap(tied(across, far_piece), "expert", 1)
    gate = gates(received, w_gate, (far_piece,))
    near = tied(jnp.stack([far_piece, first]), gate)
    far = lax.ppermute(near, plane, plane_pairs(group_count, dp_count, False))
    near_other = swap(near, "dp", 1)
    results = experts(received, gate, w_up, w_down, pages, (near,))
    results = [tied(result, theirs, far) for result in results]
    returned = exchanged(results)
    far = tied(far, results[0])
    far_other = swap(far, "dp", 1)
    mine, across_sums = project(
        tokens, theirs, latent, (near, far, near_other, far_other)
    )
    their_sums = swap(across_sums, "expert", 1)
    moe_out, carried = combine(mixing, returned, own_pages, received[1], old_latents.shape[0])
    fresh = finish(mine, their_sums, latent_gain, carried)
    latents = jnp.where((survive > 0)[:, None], carried, fresh)
    return (moe_out, latents)


def rebuild_latents(tokens, w_latent, latent_gain):
    projected = jnp.dot(
        tokens,
        lax.all_gather(w_latent, "expert", axis=0, tiled=True),
        preferred_element_type=jnp.float32,
    )
    nope_part = projected[:, :KV]
    inv_rms = lax.rsqrt(jnp.mean(nope_part * nope_part, axis=1, keepdims=True) + EPS)
    return jnp.concatenate([nope_part * inv_rms * latent_gain, projected[:, KV:]], axis=1).astype(
        jnp.bfloat16
    )


def moved_pages(old_latents, survive, old_target, rebuilt):
    peer_count = lax.axis_size("expert")
    dp_count = lax.axis_size("dp")
    page_count = old_latents.shape[0]
    per_pair = max(1, page_count // peer_count)
    slot_ids = jnp.arange(page_count, dtype=jnp.int32)
    peer_ids = jnp.arange(peer_count, dtype=jnp.int32)
    rank_ids = jnp.arange(per_pair, dtype=jnp.int32)
    valid_out = old_target >= 0
    target_peer = old_target // page_count // dp_count
    target_slot = jnp.where(valid_out, old_target % page_count + 1, 0).astype(jnp.float32)
    same_peer = (target_peer[:, None] == target_peer[None, :]) & valid_out[None, :]
    earlier = slot_ids[None, :] < slot_ids[:, None]
    out_rank = jnp.sum((same_peer & earlier).astype(jnp.int32), axis=1)
    select = (
        valid_out[None, None, :]
        & (target_peer[None, None, :] == peer_ids[:, None, None])
        & (out_rank[None, None, :] == rank_ids[None, :, None])
    )
    select = select.reshape(peer_count * per_pair, page_count)
    outgoing = jnp.dot(
        select.astype(jnp.bfloat16), old_latents, preferred_element_type=jnp.float32
    ).astype(jnp.bfloat16)
    slot_tags = jnp.dot(
        select.astype(jnp.float32), target_slot, precision=lax.Precision.HIGHEST
    ).astype(jnp.bfloat16)
    arrived, arrived_tags = (
        lax.all_to_all(
            outgoing.reshape(peer_count, per_pair, -1),
            "expert",
            split_axis=0,
            concat_axis=0,
            tiled=True,
        ),
        lax.all_to_all(
            slot_tags.reshape(peer_count, per_pair),
            "expert",
            split_axis=0,
            concat_axis=0,
            tiled=True,
        ),
    )
    tag_values = arrived_tags.reshape(peer_count * per_pair).astype(jnp.float32)
    chooser = (tag_values[None, :] == (slot_ids + 1).astype(jnp.float32)[:, None]).astype(
        jnp.bfloat16
    )
    carried = jnp.dot(
        chooser, arrived.reshape(peer_count * per_pair, -1), preferred_element_type=jnp.float32
    ).astype(jnp.bfloat16)
    return jnp.where((survive > 0)[:, None], carried, rebuilt)


def route_tables(route_ids, route_weight):
    token_count, top_count = route_ids.shape
    flat_ids = route_ids.reshape(-1)
    onehot = (flat_ids[:, None] == jnp.arange(EXPERTS, dtype=jnp.int32)[None, :]).astype(jnp.int32)
    slot_rank = jnp.sum((jnp.cumsum(onehot, axis=0) - onehot) * onehot, axis=1)
    slot_index = jnp.where(flat_ids < EXPERTS, flat_ids * CAP + slot_rank, -1)
    matches = slot_index[:, None] == jnp.arange(EXPERTS * CAP, dtype=jnp.int32)[None, :]
    matches = matches.reshape(token_count, top_count, EXPERTS * CAP)
    placing = jnp.sum(matches.astype(jnp.float32), axis=1).astype(jnp.bfloat16)
    mixing = jnp.sum(matches.astype(jnp.float32) * route_weight[:, :, None], axis=1)
    return (placing, mixing)


def expert_rows(received, w_gate, w_up, w_down, per_dev):
    unit_count = w_gate.shape[1] // per_dev
    gate_w = w_gate.reshape(w_gate.shape[0], per_dev, unit_count)
    up_w = w_up.reshape(w_up.shape[0], per_dev, unit_count)
    down_w = w_down.reshape(per_dev, unit_count, w_down.shape[1])
    gate_value = jnp.einsum("spkd,dpf->spkf", received, gate_w, preferred_element_type=jnp.float32)
    up_value = jnp.einsum("spkd,dpf->spkf", received, up_w, preferred_element_type=jnp.float32)
    hidden = (jax.nn.silu(gate_value) * up_value).astype(jnp.bfloat16)
    return jnp.einsum("spkf,pfd->spkd", hidden, down_w, preferred_element_type=jnp.float32)


def shards(
    tokens,
    w_gate,
    w_up,
    w_down,
    w_latent,
    latent_gain,
    route_ids,
    route_weight,
    old_latents,
    survive,
    old_target,
):
    rebuilt = rebuild_latents(tokens, w_latent, latent_gain).reshape(old_latents.shape[0], -1)
    latents = moved_pages(old_latents, survive, old_target, rebuilt)
    column_count = w_gate.shape[1]
    per_dev = max(1, column_count // FF)
    span_size = max(1, FF // column_count)
    group_count = EXPERTS // per_dev
    model_width = tokens.shape[1]
    placing, mixing = route_tables(route_ids, route_weight)
    outgoing = jnp.einsum("te,td->ed", placing, tokens, preferred_element_type=jnp.float32).astype(
        jnp.bfloat16
    )
    grouped = outgoing.reshape(group_count, per_dev, CAP, model_width)
    sent_rows = jnp.repeat(grouped, span_size, axis=0)
    partial_value = expert_rows(
        lax.all_to_all(sent_rows, "expert", split_axis=0, concat_axis=0, tiled=True),
        w_gate,
        w_up,
        w_down,
        per_dev,
    )
    returned = lax.all_to_all(
        partial_value.astype(jnp.bfloat16), "expert", split_axis=0, concat_axis=0, tiled=True
    ).astype(partial_value.dtype)
    summed = jnp.sum(returned.reshape(group_count, span_size, per_dev, CAP, model_width), axis=1)
    expert_out = summed.reshape(EXPERTS * CAP, model_width)
    moe_out = jnp.dot(mixing, expert_out, precision=lax.Precision.HIGHEST).astype(jnp.bfloat16)
    return (moe_out, latents)


def small_block(mesh):
    sizes = (mesh.shape["groups"], mesh.shape["expert"], mesh.shape["dp"])
    return sizes == (2, EXPERTS, 4)


def solution(mesh):
    in_specs = (
        P(("groups", "expert", "dp"), None),
        P(None, "expert"),
        P(None, "expert"),
        P("expert", None),
        P("expert", None),
        P(),
        P(("groups", "expert", "dp"), None),
        P(("groups", "expert", "dp"), None),
        P(("groups", "expert", "dp"), None),
        P(("groups", "expert", "dp")),
        P(("groups", "expert", "dp")),
    )
    out_specs = (P(("groups", "expert", "dp"), None), P(("groups", "expert", "dp"), None))
    body = block_shards if small_block(mesh) else shards
    return jax.shard_map(body, mesh=mesh, in_specs=in_specs, out_specs=out_specs, check_vma=False)
```
